512 devices in a mesh: wide: 128 (over z, y, core), narrow: 4 (over x).
Axes of the slice: x: 4, y: 8, z: 8, core: 2. Of those that a mesh axis runs over, the one named last changes fastest.
Arguments:
- features: bfloat16 [131072, 128], P('wide'), may hold values from -6 to 6
- weight: bfloat16 [128, 256], replicated, may hold values from -0.5 to 0.5
- bias: float32 [256], replicated, may hold values from -3 to 3
- cotangent: bfloat16 [131072, 256], P(('wide', 'narrow')), may hold values from -0.032958984 to 0.032958984
- tile_values: bfloat16 [128, 4, 128, 128, 128], P('wide', 'narrow'), may hold values from 0 to 0.053955078
- tile_row: int32 [128, 4, 128], P('wide', 'narrow'), may hold values from 0 to 7
- tile_source: int32 [128, 4, 128], P('wide', 'narrow'), may hold values from 0 to 127
- tile_count: int32 [128, 4], P('wide', 'narrow'), may hold values from 32 to 128, as said below
- pick: int32 [128, 4, 128], P('wide', 'narrow'), may hold values from 0 to 1
Outputs:
- hidden: bfloat16 [131072, 256], P(('wide', 'narrow'))
- grad_weight: float32 [128, 256], replicated
- grad_bias: float32 [256], replicated
The draws below stay inside these ranges and needn't reach their ends.
Inputs may be any that keep to these rules, and one draw needn't show every extreme that they name: `tile_count`: slots at or beyond a device's count are ignored; some device holds exactly 128 live slots.
All inputs are finite; a program needn't handle non-finite values.
Results may differ from the reference program's by a relative error of at most 0.0056.
Values may be sent and summed in bfloat16 or wider, within the bound.
No kernel may reach another device: no remote copies, remote signals or barrier semaphores. Data moves between devices by JAX's collectives and lax.ppermute only.
A program may use at most 64 MiB of HBM per device.

```python
import jax
import jax.numpy as jnp
from jax import lax

FIN = 128
HID = 256
TILE = 128
TR = 8
TILES = 128
ROWS = 1024
CT = 2
NODES = 131072
N_WIDE = 128
N_NARROW = 4


def draw_tile_count(key, part):
    key = jax.random.fold_in(key, 7)
    key_div, key_row, key_col = jax.random.split(key, 3)
    divisor = jax.random.randint(key_div, (N_WIDE, N_NARROW), 1, 5)
    counts = TILES // divisor
    where_row = jax.random.randint(key_row, (), 0, N_WIDE)
    where_col = jax.random.randint(key_col, (), 0, N_NARROW)
    return counts.at[where_row, where_col].set(TILES).astype(jnp.int32)


def plant(result, stream_key, smallest, top_value):
    extent = result.shape
    index_at = [jax.random.randint(jax.random.fold_in(stream_key, axis), (), 0, extent[axis]) for axis in range(len(extent))]
    result = result.at[tuple(index_at)].set(smallest)
    longest = extent.index(max(extent))
    index_at[longest] = (index_at[longest] + 1) % extent[longest]
    return result.at[tuple(index_at)].set(top_value)


def levels(own_key, shape, shards, smallest, largest):
    level, own = 1.0, jax.random.fold_in(own_key, 6)
    for dim, parts in shards:
        steps = jnp.exp(jax.random.uniform(jax.random.fold_in(own, dim), (parts,), jnp.float32, smallest / len(shards), largest / len(shards)))
        level = level * jnp.repeat(steps, shape[dim] // parts).reshape([-1 if axis == dim else 1 for axis in range(len(shape))])
    return level


def scatter_about(key, dims, scale, limit, shards=(), kind=jnp.bfloat16):
    result = scale * jax.random.normal(key, dims, jnp.float32)
    if shards:
        result = result * levels(key, dims, shards, -0.22, 0.18)
    return jnp.clip(result, -limit, limit).astype(kind)


def setup_inputs(seed: int = 0) -> dict:
    seeds = jax.random.split(jax.random.key(seed), 10)
    features = scatter_about(seeds[0], (NODES, FIN), 1.0, 6.0, ((0, 128),))
    weight = scatter_about(seeds[1], (FIN, HID), FIN ** -0.5, 0.5)
    bias = scatter_about(seeds[2], (HID,), 0.5, 3.0, (), jnp.float32)
    cotangent = scatter_about(seeds[3], (NODES, HID), (2.0 / NODES ** 0.5), 0.032958984, ((0, 512),))
    tile_values = jnp.clip(0.053955078 * jax.random.uniform(seeds[4], (N_WIDE, N_NARROW, TILES, TILE, TILE), jnp.float32) ** levels(seeds[4], (N_WIDE, N_NARROW, TILES, TILE, TILE), ((0, 128), (1, 4)), -0.2, 0.2), 0.0, 0.053955078).astype(jnp.bfloat16)
    tile_row = plant(jax.random.randint(seeds[5], (N_WIDE, N_NARROW, TILES), 0, TR), jax.random.fold_in(seeds[5], 1), 0, TR - 1).astype(jnp.int32)
    tile_source = plant(jax.random.randint(seeds[6], (N_WIDE, N_NARROW, TILES), 0, N_WIDE), jax.random.fold_in(seeds[6], 1), 0, N_WIDE - 1).astype(jnp.int32)
    tile_count = draw_tile_count(jax.random.fold_in(seeds[9], 71), 0)
    pick = plant(jax.random.randint(seeds[8], (N_WIDE, N_NARROW, N_WIDE), 0, CT), jax.random.fold_in(seeds[8], 1), 0, CT - 1).astype(jnp.int32)
    return dict(features=features, weight=weight, bias=bias, cotangent=cotangent, tile_values=tile_values, tile_row=tile_row, tile_source=tile_source, tile_count=tile_count, pick=pick)


def reference(features, weight, bias, cotangent, tile_values, tile_row, tile_source, tile_count, pick):
    feature_tiles = features.reshape(N_WIDE * TR, TILE, FIN)
    row_index = jnp.arange(TR, dtype=jnp.int32)
    slot_index = jnp.arange(TILES, dtype=jnp.int32)

    def one_block(block_args):
        block_values, block_rows, block_sources, block_counts, block_picks = block_args
        summed = jnp.zeros((TR, TILE, FIN), jnp.float32)
        for narrow_pos in range(N_NARROW):
            sources = block_sources[narrow_pos]
            column_ids = (sources * TR + narrow_pos * CT + block_picks[narrow_pos][sources]).astype(jnp.int32)
            gathered = feature_tiles[column_ids].astype(jnp.float32)
            products = jnp.einsum("tij,tjf->tif", block_values[narrow_pos].astype(jnp.float32), gathered, precision=lax.Precision.HIGHEST)
            live_mask = (slot_index < block_counts[narrow_pos]).astype(jnp.float32)
            onehot = (block_rows[narrow_pos][None, :] == row_index[:, None]).astype(jnp.float32) * live_mask[None, :]
            summed = summed + jnp.einsum("rt,tif->rif", onehot, products, precision=lax.Precision.HIGHEST)
        return summed.reshape(ROWS, FIN)

    blocks = lax.map(one_block, (tile_values, tile_row, tile_source, tile_count, pick))
    aggregated = blocks.reshape(NODES, FIN).astype(jnp.bfloat16)
    preact = jnp.dot(aggregated, weight, preferred_element_type=jnp.float32) + bias
    hidden = jax.nn.silu(preact).astype(jnp.bfloat16)
    sigmoid_pre = jax.nn.sigmoid(preact)
    dpreact = cotangent.astype(jnp.float32) * (sigmoid_pre * (1.0 + preact * (1.0 - sigmoid_pre)))
    grad_weight = jnp.dot(aggregated.T, dpreact.astype(jnp.bfloat16), preferred_element_type=jnp.float32)
    grad_bias = jnp.sum(dpreact, axis=0)
    return hidden, grad_weight, grad_bias
```

```python
import jax
import jax.numpy as jnp
from jax import lax
from jax.experimental import pallas as pl
from jax.experimental.pallas import tpu as pltpu
from jax.sharding import PartitionSpec as P

FIN = 128
HID = 256
TILE = 128
TR = 8
CT = 2
SIDE = 8
NARROW = 4
SLOTS = 128
LIST = SLOTS + TR
BF16 = jnp.bfloat16
F32 = jnp.float32


def wide_index(z, y, core):
    return (z * SIDE + y) * 2 + core


RANGE = range(SIDE)
ALONG_Y = [[[wide_index(z, y, c) for y in RANGE] for z in RANGE] for c in (0, 1)]
ALONG_Z = [[[wide_index(z, y, c) for z in RANGE] for y in RANGE] for c in (0, 1)]
FIRST = ALONG_Y[0] + ALONG_Z[1]
SECOND = ALONG_Z[0] + ALONG_Y[1]
GROUPS_Y = ALONG_Y[0] + ALONG_Y[1]
GROUPS_Z = ALONG_Z[0] + ALONG_Z[1]
COLUMN = [
    [wide_index(z, y, c) * NARROW + x for c in (0, 1) for x in range(NARROW)] for z in RANGE for y in RANGE
]
OTHER_CORE = [(i, i ^ 1) for i in range(2 * SIDE * SIDE)]


def to_all(block, axes, groups):
    return lax.all_to_all(jnp.broadcast_to(block[None], (8, *block.shape)), axes, 0, 0, axis_index_groups=groups)


def slot_list(code, core):
    source = code // 16
    valid = (code >= 0) & (source % 2 == core)
    row = code % 8
    z, y = source // 16, (source // 2) % 8
    held = jnp.where(core == 0, z * 8 + y, y * 8 + z) * 2 + (code // 8) % 2
    slot = jnp.arange(SLOTS, dtype=jnp.int32)
    rows = jnp.arange(TR, dtype=jnp.int32)
    same = (row[:, None] == row[None, :]) & valid[None, :] & (slot[None, :] < slot[:, None])
    rank = jnp.sum(same.astype(jnp.int32), axis=1)
    in_row = jnp.sum(((row[None, :] == rows[:, None]) & valid[None, :]).astype(jnp.int32), axis=1)
    padded = (in_row + 1) // 2 * 2
    place = rank + jnp.sum(jnp.where(rows[None, :] < row[:, None], padded[None, :], 0), axis=1)
    entry = 1 + slot + SLOTS * held + SLOTS * SLOTS * row
    at = jnp.arange(LIST, dtype=jnp.int32)
    hit = (place[None, :] == at[:, None]) & valid[None, :]
    entries = jnp.sum(jnp.where(hit, entry[None, :], 0), axis=1)
    return entries, jnp.sum(padded) // 2


def aggregate_kernel(core_ref, pairs_ref, own_list, other_list, own_values, other_values, held, out_ref, acc):
    core = core_ref[0]

    def run(which, entries, values):
        acc[...] = jnp.zeros_like(acc)

        def part(q):
            e = entries[q]
            live = (e > 0).astype(F32)
            e = jnp.maximum(e - 1, 0)
            tile = values[e & 127] * live.astype(BF16)
            return tile, held[(e >> 7) & 127], e >> 14

        def pair(q):
            a0, f0, row = part(2 * q)
            a1, f1, _ = part(2 * q + 1)
            prod = jnp.dot(
                jnp.concatenate([a0, a1], axis=1),
                jnp.concatenate([f0, f1], axis=0),
                preferred_element_type=F32,
            )
            return prod, row

        def step(i, carry):
            done = [pair(2 * i + u) for u in range(2)]
            for prod, row in done:
                acc[row] += prod
            return carry

        lax.fori_loop(0, (pairs_ref[which] + 1) // 2, step, 0)
        out_ref[jnp.where(which == 0, core, 1 - core)] = acc[...].astype(BF16)

    run(0, own_list, own_values)
    run(1, other_list, other_values)


def dense_kernel(parts, weight, bias, cotangent, hidden, grads):
    total = parts[0].astype(F32)
    for i in range(1, 8):
        total += parts[i].astype(F32)
    aggregated = total.astype(BF16)
    preact = jnp.dot(aggregated, weight[...], preferred_element_type=F32) + bias[...]
    sig = jax.nn.sigmoid(preact)
    hidden[...] = (preact * sig).astype(BF16)
    dpreact = cotangent[...].astype(F32) * (sig * (1.0 + preact * (1.0 - sig)))
    weight_part = lax.dot_general(
        aggregated, dpreact.astype(BF16), (((0,), (0,)), ((), ())), preferred_element_type=F32
    )
    bias_part = jnp.broadcast_to(jnp.sum(dpreact, axis=0, keepdims=True), (8, HID))
    for i in range(8):
        grads[i, 0:16, :] = weight_part[16 * i : 16 * i + 16]
        grads[i, 16:24, :] = bias_part


VMEM = pl.BlockSpec(memory_space=pltpu.VMEM)
SMEM = pl.BlockSpec(memory_space=pltpu.SMEM)


def local(features, weight, bias, cotangent, tile_values, tile_row, tile_source, tile_count, pick):
    core = lax.rem(lax.axis_index("wide"), 2)
    both = ("wide", "narrow")
    mine = lax.dynamic_slice_in_dim(features, lax.axis_index("narrow") * (CT * TILE), CT * TILE, 0)
    first = to_all(mine, "wide", FIRST).reshape(SIDE * CT * TILE, FIN)
    held = lax.all_gather(first, "wide", axis=0, tiled=True, axis_index_groups=SECOND)
    held = held.reshape(SLOTS, TILE, FIN)

    own_values = tile_values[0, 0]
    other_values = lax.ppermute(own_values, "wide", OTHER_CORE)
    source = tile_source[0, 0]
    which = source[:, None] == jnp.arange(SLOTS, dtype=jnp.int32)[None, :]
    picked = jnp.sum(jnp.where(which, pick[0, 0][None, :], 0), axis=1)
    live = jnp.arange(SLOTS, dtype=jnp.int32) < tile_count[0, 0]
    code = jnp.where(live, tile_row[0, 0] + 8 * picked + 16 * source, -1)
    other_code = lax.ppermute(code, "wide", OTHER_CORE)
    own_list, own_pairs = slot_list(code, core)
    other_list, other_pairs = slot_list(other_code, core)

    partial = pl.pallas_call(
        aggregate_kernel,
        out_shape=jax.ShapeDtypeStruct((2, TR, TILE, FIN), BF16),
        in_specs=[SMEM] * 4 + [VMEM] * 3,
        out_specs=VMEM,
        scratch_shapes=[pltpu.VMEM((TR, TILE, FIN), F32)],
        compiler_params=pltpu.CompilerParams(vmem_limit_bytes=24 << 20),
        cost_estimate=pl.CostEstimate(flops=2 * SLOTS * TILE**3, bytes_accessed=12 << 20, transcendentals=0),
        name="aggregate",
    )(core.reshape(1), jnp.stack([own_pairs, other_pairs]), own_list, other_list, own_values, other_values, held)

    rows = TR * TILE // NARROW
    parts = lax.all_to_all(partial.reshape(8, rows, FIN), both, 0, 0, axis_index_groups=COLUMN)
    hidden, grads = pl.pallas_call(
        dense_kernel,
        out_shape=(
            jax.ShapeDtypeStruct((rows, HID), BF16),
            jax.ShapeDtypeStruct((8, 24, HID), F32),
        ),
        in_specs=[VMEM] * 4,
        out_specs=(VMEM, VMEM),
        compiler_params=pltpu.CompilerParams(vmem_limit_bytes=16 << 20),
        cost_estimate=pl.CostEstimate(flops=4 * rows * FIN * HID, bytes_accessed=2 << 20, transcendentals=rows * HID),
        name="dense",
    )(parts, weight, bias.reshape(1, HID), cotangent)

    share = jnp.sum(lax.all_to_all(grads, both, 0, 0, axis_index_groups=COLUMN), axis=0)
    share = jnp.sum(to_all(share, "wide", GROUPS_Y), axis=0)
    share = jnp.sum(to_all(share, "wide", GROUPS_Z), axis=0)
    grad_weight = to_all(share[:16], both, COLUMN).reshape(FIN, HID)
    return hidden, grad_weight, share[16]


def solution(mesh):
    placed = (
        P("wide", None),
        P(),
        P(),
        P(("wide", "narrow"), None),
        P("wide", "narrow", None, None, None),
        P("wide", "narrow", None),
        P("wide", "narrow", None),
        P("wide", "narrow"),
        P("wide", "narrow", None),
    )
    return jax.shard_map(
        local,
        mesh=mesh,
        in_specs=placed,
        out_specs=(P(("wide", "narrow"), None), P(), P()),
        check_vma=False,
    )
```

```python
import jax
import jax.numpy as jnp
from jax import lax
from jax.experimental import pallas as pl
from jax.experimental.pallas import tpu as pltpu
from jax.sharding import PartitionSpec as P

FIN = 128
HID = 256
TILE = 128
TR = 8
CT = 2
SIDE = 8
NARROW = 4
SLOTS = 128
BLOCK = SIDE * CT
STEP = 4
SEGMENTS = 9
LIST = 256
SPARE = TR
BF16 = jnp.bfloat16
F32 = jnp.float32
I32 = jnp.int32


def wide_index(z, y, core):
    return (z * SIDE + y) * 2 + core


RANGE = range(SIDE)
ALONG_Y = [[[wide_index(z, y, c) for y in RANGE] for z in RANGE] for c in (0, 1)]
ALONG_Z = [[[wide_index(z, y, c) for z in RANGE] for y in RANGE] for c in (0, 1)]
FIRST = ALONG_Y[0] + ALONG_Z[1]
SECOND = ALONG_Z[0] + ALONG_Y[1]
GROUPS_Y = ALONG_Y[0] + ALONG_Y[1]
GROUPS_Z = ALONG_Z[0] + ALONG_Z[1]
COLUMN = [
    [wide_index(z, y, c) * NARROW + x for c in (0, 1) for x in range(NARROW)] for z in RANGE for y in RANGE
]
OTHER_CORE = [(i, i ^ 1) for i in range(2 * SIDE * SIDE)]


def to_all(block, axes, groups):
    return lax.all_to_all(jnp.broadcast_to(block[None], (8, *block.shape)), axes, 0, 0, axis_index_groups=groups)


def shift(block, by):
    pairs = [(ring[i], ring[(i + by) % SIDE]) for ring in SECOND for i in RANGE]
    return lax.ppermute(block, "wide", pairs)


def column(vector):
    n = vector.shape[1]
    eye = lax.broadcasted_iota(I32, (n, n), 0) == lax.broadcasted_iota(I32, (n, n), 1)
    return jnp.sum(jnp.where(eye, vector, 0), axis=1, keepdims=True)


def list_kernel(place_ref, code_ref, list_ref, start_ref):
    core, at = place_ref[0], place_ref[1]
    starts = []
    for owner in range(2):
        code = code_ref[owner : owner + 1, :]
        source = lax.shift_right_arithmetic(code, 4)
        valid = (code >= 0) & ((source & 1) == core)
        z, y = lax.shift_right_arithmetic(source, 4), lax.shift_right_arithmetic(source, 1) & 7
        along, across = jnp.where(core == 0, z, y), jnp.where(core == 0, y, z)
        tile = across * 2 + (lax.shift_right_arithmetic(code, 3) & 1)
        ahead = (along - at) & 7
        behind = 8 - ahead
        segment = jnp.where(ahead < 4, 2 * ahead, 2 * behind - 1)
        segment = jnp.where(ahead == 0, 0, segment)
        segment = jnp.where(ahead == 4, jnp.where(tile < SIDE, 7, 8), segment)
        segment = jnp.where(valid, segment, SEGMENTS)
        entry = lax.broadcasted_iota(I32, (1, SLOTS), 1) + SLOTS * tile + SLOTS * BLOCK * (code & 7)
        segments = column(segment)
        kinds = lax.broadcasted_iota(I32, (SLOTS, SLOTS), 1)
        member = (segments == kinds).astype(I32)
        sizes = jnp.sum(member, axis=0, keepdims=True)
        sizes = lax.shift_right_arithmetic(sizes + STEP - 1, 2) * STEP
        sizes = jnp.where(lax.broadcasted_iota(I32, (1, SLOTS), 1) < SEGMENTS, sizes, 0)
        size = column(sizes)
        rows = lax.broadcasted_iota(I32, (SLOTS, SLOTS), 0)
        start = jnp.sum(jnp.where(rows < kinds, size, 0), axis=0, keepdims=True)
        earlier = (segments == segment) & (rows < kinds)
        place = jnp.sum(earlier.astype(I32), axis=0, keepdims=True)
        place += jnp.sum(jnp.where(rows == segment, column(start), 0), axis=0, keepdims=True)
        place = jnp.where(valid, place, LIST)
        spare = SLOTS * BLOCK * SPARE
        places, entries = column(place), column(entry)
        slots = lax.broadcasted_iota(I32, (SLOTS, LIST), 1)
        hit = places == slots
        list_ref[owner : owner + 1, :] = spare + jnp.sum(jnp.where(hit, entries - spare, 0), axis=0, keepdims=True)
        starts.append(lax.shift_right_arithmetic(start, 2))
    for owner in range(2):
        start_ref[owner : owner + 1, :] = starts[owner]


def add_products(lists, starts, values, blocks, first, acc):
    for owner in range(2):
        for i, (block, offset) in enumerate(blocks):
            segment = first + i

            def step(k, carry, owner=owner, block=block, offset=offset):
                done = []
                for u in range(STEP):
                    e = lists[owner, k * STEP + u]
                    tile, row = (e >> 7) & (BLOCK - 1), e >> 11
                    product = jnp.dot(
                        values[owner][e & (SLOTS - 1)],
                        block[jnp.maximum(tile - offset, 0)],
                        preferred_element_type=F32,
                    )
                    done.append((row, product))
                for row, product in done:
                    acc[owner, row] += product
                return carry

            lax.fori_loop(starts[owner, segment], starts[owner, segment + 1], step, 0)


def early_kernel(lists, starts, own, other, b0, b1, b2, b3, b4, acc):
    acc[...] = jnp.zeros_like(acc)
    blocks = [(b0, 0), (b1, 0), (b2, 0), (b3, 0), (b4, 0)]
    add_products(lists, starts, (own, other), blocks, 0, acc)


def late_kernel(place, lists, starts, own, other, b5, b6, b7, b8, before, out, acc):
    acc[...] = before[...]
    blocks = [(b5, 0), (b6, 0), (b7, 0), (b8, SIDE)]
    add_products(lists, starts, (own, other), blocks, 5, acc)
    core = place[0]
    out[core] = acc[0, 0:TR].astype(BF16)
    out[1 - core] = acc[1, 0:TR].astype(BF16)


def dense_kernel(parts, weight, bias, cotangent, hidden, grads):
    total = parts[0].astype(F32)
    for i in range(1, 8):
        total += parts[i].astype(F32)
    aggregated = total.astype(BF16)
    preact = jnp.dot(aggregated, weight[...], preferred_element_type=F32) + bias[...]
    sig = jax.nn.sigmoid(preact)
    hidden[...] = (preact * sig).astype(BF16)
    dpreact = cotangent[...].astype(F32) * (sig * (1.0 + preact * (1.0 - sig)))
    weight_part = lax.dot_general(
        aggregated, dpreact.astype(BF16), (((0,), (0,)), ((), ())), preferred_element_type=F32
    ).astype(BF16)
    bias_part = jnp.sum(dpreact, axis=0, keepdims=True)
    rows = lax.broadcasted_iota(I32, (16, TILE), 0)
    left = jnp.broadcast_to(bias_part[:, :TILE], (16, TILE))
    right = jnp.broadcast_to(bias_part[:, TILE:], (16, TILE))
    biases = jnp.where(rows == 0, left, jnp.where(rows == 1, right, 0.0)).astype(BF16)
    for i in range(8):
        grads[i, 0:16, :] = weight_part[16 * i : 16 * i + 16, :TILE]
        grads[i, 16:32, :] = weight_part[16 * i : 16 * i + 16, TILE:]
        grads[i, 32:48, :] = biases


VMEM = pl.BlockSpec(memory_space=pltpu.VMEM)
SMEM = pl.BlockSpec(memory_space=pltpu.SMEM)


def total(shares):
    return jnp.sum(shares.astype(F32), axis=0)


def local(features, weight, bias, cotangent, tile_values, tile_row, tile_source, tile_count, pick):
    index = lax.axis_index("wide")
    core = lax.rem(index, 2)
    both = ("wide", "narrow")
    mine = lax.dynamic_slice_in_dim(features, lax.axis_index("narrow") * (CT * TILE), CT * TILE, 0)
    own = to_all(mine, "wide", FIRST).reshape(BLOCK, TILE, FIN)
    up2, down2 = shift(own, 2), shift(own, -2)
    up1, down1 = shift(own, 1), shift(own, -1)
    up3, down3 = shift(up2, 1), shift(down2, -1)
    up4, down4 = shift(up2[:SIDE], 2), shift(down2[SIDE:], -2)

    own_values = tile_values[0, 0]
    other_values = lax.ppermute(own_values, "wide", OTHER_CORE)
    source = tile_source[0, 0]
    which = source[:, None] == jnp.arange(SLOTS, dtype=I32)[None, :]
    picked = jnp.sum(jnp.where(which, pick[0, 0][None, :], 0), axis=1)
    live = jnp.arange(SLOTS, dtype=I32) < tile_count[0, 0]
    code = jnp.where(live, tile_row[0, 0] + 8 * picked + 16 * source, -1)[None]
    codes = jnp.concatenate([code, lax.ppermute(code, "wide", OTHER_CORE)], axis=0)
    place = jnp.stack([core, jnp.where(core == 0, index // 16, lax.rem(index // 2, 8))])
    lists, starts = pl.pallas_call(
        list_kernel,
        out_shape=(jax.ShapeDtypeStruct((2, LIST), I32), jax.ShapeDtypeStruct((2, SLOTS), I32)),
        in_specs=[SMEM, VMEM],
        out_specs=(VMEM, VMEM),
        compiler_params=pltpu.CompilerParams(vmem_limit_bytes=8 << 20),
        name="lists",
    )(place, codes)

    sums = jax.ShapeDtypeStruct((2, TR + 1, TILE, FIN), F32)
    partial = pl.pallas_call(
        early_kernel,
        out_shape=sums,
        in_specs=[SMEM] * 2 + [VMEM] * 7,
        out_specs=VMEM,
        compiler_params=pltpu.CompilerParams(vmem_limit_bytes=16 << 20),
        cost_estimate=pl.CostEstimate(flops=SLOTS * TILE**3, bytes_accessed=8 << 20, transcendentals=0),
        name="early",
    )(lists, starts, own_values, other_values, own, up1, down1, up2, down2)
    partial = pl.pallas_call(
        late_kernel,
        out_shape=jax.ShapeDtypeStruct((2, TR, TILE, FIN), BF16),
        in_specs=[SMEM] * 3 + [VMEM] * 7,
        out_specs=VMEM,
        scratch_shapes=[pltpu.VMEM(sums.shape, F32)],
        compiler_params=pltpu.CompilerParams(vmem_limit_bytes=16 << 20),
        cost_estimate=pl.CostEstimate(flops=SLOTS * TILE**3, bytes_accessed=8 << 20, transcendentals=0),
        name="late",
    )(place, lists, starts, own_values, other_values, up3, down3, up4, down4, partial)

    rows = TR * TILE // NARROW
    parts = lax.all_to_all(partial.reshape(8, rows, FIN), both, 0, 0, axis_index_groups=COLUMN)
    hidden, grads = pl.pallas_call(
        dense_kernel,
        out_shape=(
            jax.ShapeDtypeStruct((rows, HID), BF16),
            jax.ShapeDtypeStruct((8, 48, TILE), BF16),
        ),
        in_specs=[VMEM] * 4,
        out_specs=(VMEM, VMEM),
        compiler_params=pltpu.CompilerParams(vmem_limit_bytes=16 << 20),
        cost_estimate=pl.CostEstimate(flops=4 * rows * FIN * HID, bytes_accessed=2 << 20, transcendentals=rows * HID),
        name="dense",
    )(parts, weight, bias.reshape(1, HID), cotangent)

    share = total(lax.all_to_all(grads, both, 0, 0, axis_index_groups=COLUMN)).astype(BF16)
    share = total(to_all(share, "wide", GROUPS_Y)).astype(BF16)
    share = total(to_all(share, "wide", GROUPS_Z))
    chunk = jnp.concatenate([share[0:16], share[16:32]], axis=1)
    grad_weight = to_all(chunk, both, COLUMN).reshape(FIN, HID)
    return hidden, grad_weight, share[32:34].reshape(HID)


def solution(mesh):
    placed = (
        P("wide", None),
        P(),
        P(),
        P(("wide", "narrow"), None),
        P("wide", "narrow", None, None, None),
        P("wide", "narrow", None),
        P("wide", "narrow", None),
        P("wide", "narrow"),
        P("wide", "narrow", None),
    )
    return jax.shard_map(
        local,
        mesh=mesh,
        in_specs=placed,
        out_specs=(P(("wide", "narrow"), None), P(), P()),
        check_vma=False,
    )
```

```python
import jax
import jax.numpy as jnp
from jax import lax
from jax.experimental import pallas as pl
from jax.experimental.pallas import tpu as pltpu
from jax.sharding import PartitionSpec as P

FIN = 128
HID = 256
TILE = 128
TR = 8
CT = 2
SIDE = 8
NARROW = 4
SLOTS = 128
BLOCK = SIDE * CT
STEP = 4
SEGMENTS = 8
LIST = 256
HELD = SLOTS + (STEP - 1) * SEGMENTS + STEP
SPARE = TR
BF16 = jnp.bfloat16
F32 = jnp.float32
I32 = jnp.int32


def wide_index(z, y, core):
    return (z * SIDE + y) * 2 + core


RANGE = range(SIDE)
ALONG_Y = [[[wide_index(z, y, c) for y in RANGE] for z in RANGE] for c in (0, 1)]
ALONG_Z = [[[wide_index(z, y, c) for z in RANGE] for y in RANGE] for c in (0, 1)]
FIRST = ALONG_Y[0] + ALONG_Z[1]
SECOND = ALONG_Z[0] + ALONG_Y[1]
GROUPS_Y = ALONG_Y[0] + ALONG_Y[1]
GROUPS_Z = ALONG_Z[0] + ALONG_Z[1]
COLUMN = [
    [wide_index(z, y, c) * NARROW + x for c in (0, 1) for x in range(NARROW)] for z in RANGE for y in RANGE
]
OTHER_CORE = [(i, i ^ 1) for i in range(2 * SIDE * SIDE)]


def to_all(block, axes, groups):
    return lax.all_to_all(jnp.broadcast_to(block[None], (8, *block.shape)), axes, 0, 0, axis_index_groups=groups)


def shift(block, by):
    pairs = [(ring[i], ring[(i + by) % SIDE]) for ring in SECOND for i in RANGE]
    return lax.ppermute(block, "wide", pairs)


def column(vector):
    n = vector.shape[1]
    eye = lax.broadcasted_iota(I32, (n, n), 0) == lax.broadcasted_iota(I32, (n, n), 1)
    return jnp.sum(jnp.where(eye, vector, 0), axis=1, keepdims=True)


def list_kernel(place_ref, code_ref, list_ref, start_ref):
    core, at = place_ref[0], place_ref[1]
    starts = []
    for owner in range(2):
        code = code_ref[owner : owner + 1, :]
        source = lax.shift_right_arithmetic(code, 4)
        valid = (code >= 0) & ((source & 1) == core)
        z, y = lax.shift_right_arithmetic(source, 4), lax.shift_right_arithmetic(source, 1) & 7
        along, across = jnp.where(core == 0, z, y), jnp.where(core == 0, y, z)
        tile = across * 2 + (lax.shift_right_arithmetic(code, 3) & 1)
        ahead = (along - at) & 7
        behind = 8 - ahead
        segment = jnp.where(ahead < 4, 2 * ahead, 2 * behind - 1)
        segment = jnp.where(ahead == 0, 0, segment)
        segment = jnp.where(ahead == 4, 7, segment)
        segment = jnp.where(valid, segment, SEGMENTS)
        entry = lax.broadcasted_iota(I32, (1, SLOTS), 1) + SLOTS * tile + SLOTS * BLOCK * (code & 7)
        segments = column(segment)
        kinds = lax.broadcasted_iota(I32, (SLOTS, SLOTS), 1)
        member = (segments == kinds).astype(I32)
        sizes = jnp.sum(member, axis=0, keepdims=True)
        sizes = lax.shift_right_arithmetic(sizes + STEP - 1, 2) * STEP
        sizes = jnp.where(lax.broadcasted_iota(I32, (1, SLOTS), 1) < SEGMENTS, sizes, 0)
        size = column(sizes)
        rows = lax.broadcasted_iota(I32, (SLOTS, SLOTS), 0)
        start = jnp.sum(jnp.where(rows < kinds, size, 0), axis=0, keepdims=True)
        earlier = (segments == segment) & (rows < kinds)
        place = jnp.sum(earlier.astype(I32), axis=0, keepdims=True)
        place += jnp.sum(jnp.where(rows == segment, column(start), 0), axis=0, keepdims=True)
        place = jnp.where(valid, place, LIST)
        spare = SLOTS * BLOCK * SPARE
        places, entries = column(place), column(entry)
        slots = lax.broadcasted_iota(I32, (SLOTS, LIST), 1)
        hit = places == slots
        list_ref[owner : owner + 1, :] = spare + jnp.sum(jnp.where(hit, entries - spare, 0), axis=0, keepdims=True)
        starts.append(lax.shift_right_arithmetic(start, 2))
    for owner in range(2):
        start_ref[owner : owner + 1, :] = starts[owner]


def add_products(lists, starts, values, blocks, first, acc, held, sems):
    def tiles(owner, i, wait):
        base = starts[owner, first]

        def step(k, carry):
            for u in range(STEP):
                slot = lists[owner, k * STEP + u] & (SLOTS - 1)
                at = (k - base) * STEP + u
                copy = pltpu.make_async_copy(values[owner].at[slot], held.at[owner, at], sems.at[owner, i])
                if wait:
                    copy.wait()
                else:
                    copy.start()
            return carry

        lax.fori_loop(starts[owner, first + i], starts[owner, first + i + 1], step, 0)

    def multiply(owner, i, block):
        base = starts[owner, first]

        def step(k, carry):
            done = []
            for u in range(STEP):
                e = lists[owner, k * STEP + u]
                tile, row = (e >> 7) & (BLOCK - 1), e >> 11
                product = jnp.dot(held[owner, (k - base) * STEP + u], block[tile], preferred_element_type=F32)
                done.append((row, product))
            for row, product in done:
                acc[owner, row] += product
            return carry

        lax.fori_loop(starts[owner, first + i], starts[owner, first + i + 1], step, 0)

    todo = [(owner, i, block) for i, block in enumerate(blocks) for owner in range(2)]
    for owner, i, _ in todo:
        tiles(owner, i, False)
    yield
    for owner, i, block in todo:
        tiles(owner, i, True)
        multiply(owner, i, block)


def early_kernel(lists, starts, own, other, b0, b1, b2, b3, b4, acc, held, sems):
    for _ in add_products(lists, starts, (own, other), (b0, b1, b2, b3, b4), 0, acc, held, sems):
        acc[...] = jnp.zeros_like(acc)


def late_kernel(place, lists, starts, own, other, b5, b6, b7, before, out, acc, held, sems):
    for _ in add_products(lists, starts, (own, other), (b5, b6, b7), 5, acc, held, sems):
        acc[...] = before[...]
    core = place[0]
    out[core] = acc[0, 0:TR].astype(BF16)
    out[1 - core] = acc[1, 0:TR].astype(BF16)


def dense_kernel(parts, weight, bias, cotangent, hidden, grads):
    total = parts[0].astype(F32)
    for i in range(1, 8):
        total += parts[i].astype(F32)
    aggregated = total.astype(BF16)
    preact = jnp.dot(aggregated, weight[...], preferred_element_type=F32) + bias[...]
    sig = jax.nn.sigmoid(preact)
    hidden[...] = (preact * sig).astype(BF16)
    dpreact = cotangent[...].astype(F32) * (sig * (1.0 + preact * (1.0 - sig)))
    weight_part = lax.dot_general(
        aggregated, dpreact.astype(BF16), (((0,), (0,)), ((), ())), preferred_element_type=F32
    ).astype(BF16)
    bias_part = jnp.sum(dpreact, axis=0, keepdims=True)
    rows = lax.broadcasted_iota(I32, (16, TILE), 0)
    left = jnp.broadcast_to(bias_part[:, :TILE], (16, TILE))
    right = jnp.broadcast_to(bias_part[:, TILE:], (16, TILE))
    biases = jnp.where(rows == 0, left, jnp.where(rows == 1, right, 0.0)).astype(BF16)
    for i in range(8):
        grads[i, 0:16, :] = weight_part[16 * i : 16 * i + 16, :TILE]
        grads[i, 16:32, :] = weight_part[16 * i : 16 * i + 16, TILE:]
        grads[i, 32:48, :] = biases


VMEM = pl.BlockSpec(memory_space=pltpu.VMEM)
SMEM = pl.BlockSpec(memory_space=pltpu.SMEM)
HBM = pl.BlockSpec(memory_space=pltpu.HBM)


def total(shares):
    return jnp.sum(shares.astype(F32), axis=0)


def local(features, weight, bias, cotangent, tile_values, tile_row, tile_source, tile_count, pick):
    index = lax.axis_index("wide")
    core = lax.rem(index, 2)
    both = ("wide", "narrow")
    mine = lax.dynamic_slice_in_dim(features, lax.axis_index("narrow") * (CT * TILE), CT * TILE, 0)
    own_values = tile_values[0, 0]
    other_values = lax.ppermute(own_values, "wide", OTHER_CORE)
    own = to_all(mine, "wide", FIRST).reshape(BLOCK, TILE, FIN)
    own, other_values = lax.optimization_barrier((own, other_values))
    up2, down2 = shift(own, 2), shift(own, -2)
    up1, down1 = shift(own, 1), shift(own, -1)
    up3, down3 = shift(up2, 1), shift(down2, -1)
    far = shift(own, 4)

    source = tile_source[0, 0]
    which = source[:, None] == jnp.arange(SLOTS, dtype=I32)[None, :]
    picked = jnp.sum(jnp.where(which, pick[0, 0][None, :], 0), axis=1)
    live = jnp.arange(SLOTS, dtype=I32) < tile_count[0, 0]
    code = jnp.where(live, tile_row[0, 0] + 8 * picked + 16 * source, -1)[None]
    codes = jnp.concatenate([code, lax.ppermute(code, "wide", OTHER_CORE)], axis=0)
    place = jnp.stack([core, jnp.where(core == 0, index // 16, lax.rem(index // 2, 8))])
    lists, starts = pl.pallas_call(
        list_kernel,
        out_shape=(jax.ShapeDtypeStruct((2, LIST), I32), jax.ShapeDtypeStruct((2, SLOTS), I32)),
        in_specs=[SMEM, VMEM],
        out_specs=(VMEM, VMEM),
        compiler_params=pltpu.CompilerParams(vmem_limit_bytes=8 << 20),
        name="lists",
    )(place, codes)

    sums = jax.ShapeDtypeStruct((2, TR + 1, TILE, FIN), F32)
    partial = pl.pallas_call(
        early_kernel,
        out_shape=sums,
        in_specs=[SMEM] * 2 + [HBM] * 2 + [VMEM] * 5,
        out_specs=VMEM,
        scratch_shapes=[pltpu.VMEM((2, HELD, TILE, TILE), BF16), pltpu.SemaphoreType.DMA((2, 5))],
        compiler_params=pltpu.CompilerParams(vmem_limit_bytes=24 << 20),
        cost_estimate=pl.CostEstimate(flops=SLOTS * TILE**3, bytes_accessed=8 << 20, transcendentals=0),
        name="early",
    )(lists, starts, own_values, other_values, own, up1, down1, up2, down2)
    partial = pl.pallas_call(
        late_kernel,
        out_shape=jax.ShapeDtypeStruct((2, TR, TILE, FIN), BF16),
        in_specs=[SMEM] * 3 + [HBM] * 2 + [VMEM] * 4,
        out_specs=VMEM,
        scratch_shapes=[
            pltpu.VMEM(sums.shape, F32),
            pltpu.VMEM((2, HELD, TILE, TILE), BF16),
            pltpu.SemaphoreType.DMA((2, 3)),
        ],
        compiler_params=pltpu.CompilerParams(vmem_limit_bytes=24 << 20),
        cost_estimate=pl.CostEstimate(flops=SLOTS * TILE**3, bytes_accessed=8 << 20, transcendentals=0),
        name="late",
    )(place, lists, starts, own_values, other_values, up3, down3, far, partial)

    rows = TR * TILE // NARROW
    parts = lax.all_to_all(partial.reshape(8, rows, FIN), both, 0, 0, axis_index_groups=COLUMN)
    hidden, grads = pl.pallas_call(
        dense_kernel,
        out_shape=(
            jax.ShapeDtypeStruct((rows, HID), BF16),
            jax.ShapeDtypeStruct((8, 48, TILE), BF16),
        ),
        in_specs=[VMEM] * 4,
        out_specs=(VMEM, VMEM),
        compiler_params=pltpu.CompilerParams(vmem_limit_bytes=16 << 20),
        cost_estimate=pl.CostEstimate(flops=4 * rows * FIN * HID, bytes_accessed=2 << 20, transcendentals=rows * HID),
        name="dense",
    )(parts, weight, bias.reshape(1, HID), cotangent)

    share = total(lax.all_to_all(grads, both, 0, 0, axis_index_groups=COLUMN))[:40]
    share = total(to_all(share, "wide", GROUPS_Y))
    share = total(to_all(share, "wide", GROUPS_Z))
    chunk = jnp.concatenate([share[0:16], share[16:32]], axis=1)
    grad_weight = to_all(chunk, both, COLUMN).reshape(FIN, HID)
    return hidden, grad_weight, share[32:34].reshape(HID)


def solution(mesh):
    placed = (
        P("wide", None),
        P(),
        P(),
        P(("wide", "narrow"), None),
        P("wide", "narrow", None, None, None),
        P("wide", "narrow", None),
        P("wide", "narrow", None),
        P("wide", "narrow"),
        P("wide", "narrow", None),
    )
    return jax.shard_map(
        local,
        mesh=mesh,
        in_specs=placed,
        out_specs=(P(("wide", "narrow"), None), P(), P()),
        check_vma=False,
    )
```

```python
import jax
import jax.numpy as jnp
from jax import lax
from jax.experimental import pallas as pl
from jax.experimental.pallas import tpu as pltpu
from jax.sharding import PartitionSpec as P

FIN = 128
HID = 256
TILE = 128
TR = 8
CT = 2
SIDE = 8
NARROW = 4
SLOTS = 128
BLOCK = SIDE * CT
STEP = 8
SEGMENTS = 8
FAR = 5
LIST = 256
SPARE = TR
BF16 = jnp.bfloat16
F32 = jnp.float32
I32 = jnp.int32


def wide_index(z, y, core):
    return (z * SIDE + y) * 2 + core


RANGE = range(SIDE)
ALONG_Y = [[[wide_index(z, y, c) for y in RANGE] for z in RANGE] for c in (0, 1)]
ALONG_Z = [[[wide_index(z, y, c) for z in RANGE] for y in RANGE] for c in (0, 1)]
FIRST = ALONG_Y[0] + ALONG_Z[1]
SECOND = ALONG_Z[0] + ALONG_Y[1]
GROUPS_Y = ALONG_Y[0] + ALONG_Y[1]
GROUPS_Z = ALONG_Z[0] + ALONG_Z[1]
COLUMN = [
    [wide_index(z, y, c) * NARROW + x for c in (0, 1) for x in range(NARROW)] for z in RANGE for y in RANGE
]
CHIP = [[2 * i, 2 * i + 1] for i in range(SIDE * SIDE)]
OTHER_CORE = [(i, i ^ 1) for i in range(2 * SIDE * SIDE)]


def to_all(block, axes, groups):
    return lax.all_to_all(jnp.broadcast_to(block[None], (8, *block.shape)), axes, 0, 0, axis_index_groups=groups)


def shift(block, by):
    pairs = [(ring[i], ring[(i + by) % SIDE]) for ring in SECOND for i in RANGE]
    return lax.ppermute(block, "wide", pairs)


def column(vector):
    n = vector.shape[1]
    eye = lax.broadcasted_iota(I32, (n, n), 0) == lax.broadcasted_iota(I32, (n, n), 1)
    return jnp.sum(jnp.where(eye, vector, 0), axis=1, keepdims=True)


def list_kernel(place_ref, code_ref, list_ref, start_ref):
    core, at = place_ref[0], place_ref[1]
    starts = []
    for owner in range(2):
        code = jnp.where(core == owner, code_ref[0:1, :], code_ref[1:2, :])
        source = lax.shift_right_arithmetic(code, 4)
        valid = (code >= 0) & ((source & 1) == core)
        z, y = lax.shift_right_arithmetic(source, 4), lax.shift_right_arithmetic(source, 1) & 7
        along, across = jnp.where(core == 0, z, y), jnp.where(core == 0, y, z)
        tile = across * 2 + (lax.shift_right_arithmetic(code, 3) & 1)
        ahead = (along - at) & 7
        behind = 8 - ahead
        segment = jnp.where(ahead < 4, 2 * ahead, 2 * behind - 1)
        segment = jnp.where(ahead == 0, 0, segment)
        segment = jnp.where(segment < FAR, segment, segment + 1)
        segment = jnp.where(ahead == 4, FAR, segment)
        segment = jnp.where(valid, segment, SEGMENTS)
        entry = lax.broadcasted_iota(I32, (1, SLOTS), 1) + SLOTS * tile + SLOTS * BLOCK * (code & 7)
        segments = column(segment)
        kinds = lax.broadcasted_iota(I32, (SLOTS, SLOTS), 1)
        member = (segments == kinds).astype(I32)
        sizes = jnp.sum(member, axis=0, keepdims=True)
        sizes = lax.shift_right_arithmetic(sizes + STEP - 1, 3) * STEP
        sizes = jnp.where(lax.broadcasted_iota(I32, (1, SLOTS), 1) < SEGMENTS, sizes, 0)
        size = column(sizes)
        rows = lax.broadcasted_iota(I32, (SLOTS, SLOTS), 0)
        start = jnp.sum(jnp.where(rows < kinds, size, 0), axis=0, keepdims=True)
        earlier = (segments == segment) & (rows < kinds)
        place = jnp.sum(earlier.astype(I32), axis=0, keepdims=True)
        place += jnp.sum(jnp.where(rows == segment, column(start), 0), axis=0, keepdims=True)
        place = jnp.where(valid, place, LIST)
        spare = SLOTS * BLOCK * SPARE
        places, entries = column(place), column(entry)
        slots = lax.broadcasted_iota(I32, (SLOTS, LIST), 1)
        hit = places == slots
        list_ref[owner : owner + 1, :] = spare + jnp.sum(jnp.where(hit, entries - spare, 0), axis=0, keepdims=True)
        starts.append(lax.shift_right_arithmetic(start, 3))
    for owner in range(2):
        start_ref[owner : owner + 1, :] = starts[owner]


def add_products(lists, starts, owner, values, blocks, first, acc):
    for i, block in enumerate(blocks):

        def step(k, carry, block=block):
            done = []
            for u in range(STEP):
                e = lists[owner, k * STEP + u]
                tile, row = (e >> 7) & (BLOCK - 1), e >> 11
                done.append((row, jnp.dot(values[e & (SLOTS - 1)], block[tile], preferred_element_type=F32)))
            for row, product in done:
                acc[owner, row] += product
            return carry

        lax.fori_loop(starts[owner, first + i], starts[owner, first + i + 1], step, 0)


def early_kernel(lists, starts, own, other, b0, b1, b2, b3, b4, b5, acc, other_here, sem):
    copy = pltpu.make_async_copy(other, other_here, sem)
    copy.start()
    acc[...] = jnp.zeros_like(acc)
    blocks = (b0, b1, b2, b3, b4, b5)
    add_products(lists, starts, 0, own, blocks, 0, acc)
    copy.wait()
    add_products(lists, starts, 1, other_here, blocks, 0, acc)


def late_kernel(place, lists, starts, own, other, b6, b7, before, out, acc):
    acc[...] = before[...]
    add_products(lists, starts, 0, own, (b6, b7), 6, acc)
    add_products(lists, starts, 1, other, (b6, b7), 6, acc)
    core = place[0]
    out[core] = acc[0, 0:TR].astype(BF16)
    out[1 - core] = acc[1, 0:TR].astype(BF16)


def dense_kernel(parts, weight, bias, cotangent, hidden, grads):
    total = parts[0].astype(F32)
    for i in range(1, 8):
        total += parts[i].astype(F32)
    aggregated = total.astype(BF16)
    preact = jnp.dot(aggregated, weight[...], preferred_element_type=F32) + bias[...]
    sig = jax.nn.sigmoid(preact)
    hidden[...] = (preact * sig).astype(BF16)
    dpreact = cotangent[...].astype(F32) * (sig * (1.0 + preact * (1.0 - sig)))
    weight_part = lax.dot_general(
        aggregated, dpreact.astype(BF16), (((0,), (0,)), ((), ())), preferred_element_type=F32
    ).astype(BF16)
    bias_part = jnp.sum(dpreact, axis=0, keepdims=True)
    rows = lax.broadcasted_iota(I32, (16, TILE), 0)
    left = jnp.broadcast_to(bias_part[:, :TILE], (16, TILE))
    right = jnp.broadcast_to(bias_part[:, TILE:], (16, TILE))
    biases = jnp.where(rows == 0, left, jnp.where(rows == 1, right, 0.0)).astype(BF16)
    for i in range(8):
        grads[i, 0:16, :] = weight_part[16 * i : 16 * i + 16, :TILE]
        grads[i, 16:32, :] = weight_part[16 * i : 16 * i + 16, TILE:]
        grads[i, 32:48, :] = biases


VMEM = pl.BlockSpec(memory_space=pltpu.VMEM)
SMEM = pl.BlockSpec(memory_space=pltpu.SMEM)
HBM = pl.BlockSpec(memory_space=pltpu.HBM)


def total(shares):
    return jnp.sum(shares.astype(F32), axis=0)


def local(features, weight, bias, cotangent, tile_values, tile_row, tile_source, tile_count, pick):
    index = lax.axis_index("wide")
    core = lax.rem(index, 2)
    both = ("wide", "narrow")
    mine = lax.dynamic_slice_in_dim(features, lax.axis_index("narrow") * (CT * TILE), CT * TILE, 0)
    own_values = tile_values[0, 0]
    other_values = lax.ppermute(own_values, "wide", OTHER_CORE)
    own = to_all(mine, "wide", FIRST).reshape(BLOCK, TILE, FIN)
    own, other_values = lax.optimization_barrier((own, other_values))
    up2, down2 = shift(own, 2), shift(own, -2)
    up1, down1 = shift(own, 1), shift(own, -1)
    up3, down3 = shift(up2, 1), shift(down2, -1)
    far = shift(own, 4)

    source = tile_source[0, 0]
    which = source[:, None] == jnp.arange(SLOTS, dtype=I32)[None, :]
    picked = jnp.sum(jnp.where(which, pick[0, 0][None, :], 0), axis=1)
    live = jnp.arange(SLOTS, dtype=I32) < tile_count[0, 0]
    code = jnp.where(live, tile_row[0, 0] + 8 * picked + 16 * source, -1)[None]
    codes = lax.all_to_all(jnp.broadcast_to(code, (2, SLOTS)), "wide", 0, 0, axis_index_groups=CHIP)
    place = jnp.stack([core, jnp.where(core == 0, index // 16, lax.rem(index // 2, 8))])
    lists, starts = pl.pallas_call(
        list_kernel,
        out_shape=(jax.ShapeDtypeStruct((2, LIST), I32), jax.ShapeDtypeStruct((2, SLOTS), I32)),
        in_specs=[SMEM, VMEM],
        out_specs=(VMEM, VMEM),
        compiler_params=pltpu.CompilerParams(vmem_limit_bytes=8 << 20),
        name="lists",
    )(place, codes)

    sums = jax.ShapeDtypeStruct((2, TR + 1, TILE, FIN), F32)
    partial, other_here = pl.pallas_call(
        early_kernel,
        out_shape=(sums, jax.ShapeDtypeStruct(own_values.shape, BF16)),
        in_specs=[SMEM] * 2 + [VMEM, HBM] + [VMEM] * 6,
        out_specs=(VMEM, VMEM),
        scratch_shapes=[pltpu.SemaphoreType.DMA],
        compiler_params=pltpu.CompilerParams(vmem_limit_bytes=16 << 20),
        cost_estimate=pl.CostEstimate(flops=SLOTS * TILE**3, bytes_accessed=8 << 20, transcendentals=0),
        name="early",
    )(lists, starts, own_values, other_values, own, up1, down1, up2, down2, far)
    partial = pl.pallas_call(
        late_kernel,
        out_shape=jax.ShapeDtypeStruct((2, TR, TILE, FIN), BF16),
        in_specs=[SMEM] * 3 + [VMEM] * 5,
        out_specs=VMEM,
        scratch_shapes=[pltpu.VMEM(sums.shape, F32)],
        compiler_params=pltpu.CompilerParams(vmem_limit_bytes=16 << 20),
        cost_estimate=pl.CostEstimate(flops=SLOTS * TILE**3, bytes_accessed=8 << 20, transcendentals=0),
        name="late",
    )(place, lists, starts, own_values, other_here, up3, down3, partial)

    rows = TR * TILE // NARROW
    parts = lax.all_to_all(partial.reshape(8, rows, FIN), both, 0, 0, axis_index_groups=COLUMN)
    hidden, grads = pl.pallas_call(
        dense_kernel,
        out_shape=(
            jax.ShapeDtypeStruct((rows, HID), BF16),
            jax.ShapeDtypeStruct((8, 48, TILE), BF16),
        ),
        in_specs=[VMEM] * 4,
        out_specs=(VMEM, VMEM),
        compiler_params=pltpu.CompilerParams(vmem_limit_bytes=16 << 20),
        cost_estimate=pl.CostEstimate(flops=4 * rows * FIN * HID, bytes_accessed=2 << 20, transcendentals=rows * HID),
        name="dense",
    )(parts, weight, bias.reshape(1, HID), cotangent)

    share = total(lax.all_to_all(grads, both, 0, 0, axis_index_groups=COLUMN))[:40]
    share = total(to_all(share, "wide", GROUPS_Y))
    share = total(to_all(share, "wide", GROUPS_Z))
    chunk = jnp.concatenate([share[0:16], share[16:32]], axis=1)
    grad_weight = to_all(chunk, both, COLUMN).reshape(FIN, HID)
    return hidden, grad_weight, share[32:34].reshape(HID)


def solution(mesh):
    placed = (
        P("wide", None),
        P(),
        P(),
        P(("wide", "narrow"), None),
        P("wide", "narrow", None, None, None),
        P("wide", "narrow", None),
        P("wide", "narrow", None),
        P("wide", "narrow"),
        P("wide", "narrow", None),
    )
    return jax.shard_map(
        local,
        mesh=mesh,
        in_specs=placed,
        out_specs=(P(("wide", "narrow"), None), P(), P()),
        check_vma=False,
    )
```

```python
import jax
import jax.numpy as jnp
from jax import lax
from jax.experimental import pallas as pl
from jax.experimental.pallas import tpu as pltpu
from jax.sharding import PartitionSpec as P

FIN = 128
HID = 256
TILE = 128
TR = 8
CT = 2
SIDE = 8
NARROW = 4
SLOTS = 128
BLOCK = SIDE * CT
STEP = 8
SEGMENTS = 8
EARLY = 5
LIST = 256
SPARE = TR
BF16 = jnp.bfloat16
F32 = jnp.float32
I32 = jnp.int32


def wide_index(z, y, core):
    return (z * SIDE + y) * 2 + core


RANGE = range(SIDE)
ALONG_Y = [[[wide_index(z, y, c) for y in RANGE] for z in RANGE] for c in (0, 1)]
ALONG_Z = [[[wide_index(z, y, c) for z in RANGE] for y in RANGE] for c in (0, 1)]
FIRST = ALONG_Y[0] + ALONG_Z[1]
SECOND = ALONG_Z[0] + ALONG_Y[1]
GROUPS_Y = ALONG_Y[0] + ALONG_Y[1]
GROUPS_Z = ALONG_Z[0] + ALONG_Z[1]
COLUMN = [
    [wide_index(z, y, c) * NARROW + x for c in (0, 1) for x in range(NARROW)] for z in RANGE for y in RANGE
]
OTHER_CORE = [(i, i ^ 1) for i in range(2 * SIDE * SIDE)]


def to_all(block, axes, groups):
    return lax.all_to_all(jnp.broadcast_to(block[None], (8, *block.shape)), axes, 0, 0, axis_index_groups=groups)


def shift(block, by):
    pairs = [(line[i], line[(i + (by if i % 2 == 0 else -by)) % SIDE]) for line in SECOND for i in RANGE]
    return lax.ppermute(block, "wide", pairs)


def column(vector):
    n = vector.shape[1]
    eye = lax.broadcasted_iota(I32, (n, n), 0) == lax.broadcasted_iota(I32, (n, n), 1)
    return jnp.sum(jnp.where(eye, vector, 0), axis=1, keepdims=True)


def make_list(place, slots):
    core, at = place[0], place[1]
    code, pick = slots[0:1], slots[1:2]
    source = lax.shift_right_arithmetic(code, 3)
    valid = (code >= 0) & ((source & 1) == core)
    rows = lax.broadcasted_iota(I32, (SLOTS, SLOTS), 0)
    kinds = lax.broadcasted_iota(I32, (SLOTS, SLOTS), 1)
    lanes = lax.broadcasted_iota(I32, (1, SLOTS), 1)
    picked = jnp.sum(jnp.where(rows == source, column(pick), 0), axis=0, keepdims=True)
    z, y = lax.shift_right_arithmetic(source, 4), lax.shift_right_arithmetic(source, 1) & 7
    along, across = jnp.where(core == 0, z, y), jnp.where(core == 0, y, z)
    tile = across * 2 + picked
    ahead = jnp.where(at % 2 == 0, along - at, at - along) & 7
    segment = jnp.zeros_like(ahead)
    for kind, distance in enumerate((1, 7, 6, 2, 3, 5, 4)):
        segment = jnp.where(ahead == distance, kind + 1, segment)
    segment = jnp.where(valid, segment, SEGMENTS)
    entry = lanes + SLOTS * tile + SLOTS * BLOCK * (code & 7)
    segments = column(segment)
    sizes = jnp.sum((segments == kinds).astype(I32), axis=0, keepdims=True)
    sizes = lax.shift_right_arithmetic(sizes + STEP - 1, 3) * STEP
    size = column(jnp.where(lanes < SEGMENTS, sizes, 0))
    start = jnp.sum(jnp.where(rows < kinds, size, 0), axis=0, keepdims=True)
    earlier = (segments == segment) & (rows < kinds)
    place_of = jnp.sum(earlier.astype(I32), axis=0, keepdims=True)
    place_of += jnp.sum(jnp.where(rows == segment, column(start), 0), axis=0, keepdims=True)
    place_of = jnp.where(valid, place_of, LIST)
    spare = SLOTS * BLOCK * SPARE
    hit = column(place_of) == lax.broadcasted_iota(I32, (SLOTS, LIST), 1)
    entries = spare + jnp.sum(jnp.where(hit, column(entry) - spare, 0), axis=0, keepdims=True)
    return entries, lax.shift_right_arithmetic(start, 3)


def add_products(entries, starts, owner, values, blocks, first, acc):
    for i, block in enumerate(blocks):

        def step(k, carry, block=block):
            done = []
            for u in range(STEP):
                e = entries[owner, k * STEP + u]
                tile, row = (e >> 7) & (BLOCK - 1), e >> 11
                done.append((row, jnp.dot(values[e & (SLOTS - 1)], block[tile], preferred_element_type=F32)))
            for row, product in done:
                acc[row] += product
            return carry

        lax.fori_loop(starts[owner, first + i], starts[owner, first + i + 1], step, 0)


def own_kernel(place, slots, own, other, b0, b1, b2, b3, b4, acc, own_here, other_here, lists, starts, entries, bounds, sems):
    copies = [
        pltpu.make_async_copy(own, own_here, sems.at[0]),
        pltpu.make_async_copy(other, other_here, sems.at[1]),
    ]
    copies[0].start()
    copies[1].start()
    lists[...], starts[...] = make_list(place, slots[...])
    scalars = [
        pltpu.make_async_copy(lists, entries, sems.at[2]),
        pltpu.make_async_copy(starts, bounds, sems.at[3]),
    ]
    scalars[0].start()
    scalars[1].start()
    acc[...] = jnp.zeros_like(acc)
    scalars[0].wait()
    scalars[1].wait()
    copies[0].wait()
    add_products(entries, bounds, 0, own_here, (b0, b1, b2, b3, b4), 0, acc)
    copies[1].wait()


def other_kernel(place, slots, other, own_list, own_start, b0, b1, b2, b3, b4, acc, lists, starts, entries, bounds, sems):
    lists[0:1, :], starts[0:1, :] = own_list[...], own_start[...]
    lists[1:2, :], starts[1:2, :] = make_list(place, slots[...])
    scalars = [
        pltpu.make_async_copy(lists, entries, sems.at[0]),
        pltpu.make_async_copy(starts, bounds, sems.at[1]),
    ]
    scalars[0].start()
    scalars[1].start()
    acc[...] = jnp.zeros_like(acc)
    scalars[0].wait()
    scalars[1].wait()
    add_products(entries, bounds, 1, other, (b0, b1, b2, b3, b4), 0, acc)


def late_kernel(place, lists, starts, own, other, b5, b6, b7, own_before, other_before, out, own_acc, other_acc):
    own_acc[...] = own_before[...]
    other_acc[...] = other_before[...]
    add_products(lists, starts, 0, own, (b5, b6, b7), EARLY, own_acc)
    add_products(lists, starts, 1, other, (b5, b6, b7), EARLY, other_acc)
    core = place[0]
    out[core] = own_acc[0:TR].astype(BF16)
    out[1 - core] = other_acc[0:TR].astype(BF16)


def dense_kernel(parts, weight, bias, cotangent, hidden, grads):
    total = parts[0].astype(F32)
    for i in range(1, 8):
        total += parts[i].astype(F32)
    aggregated = total.astype(BF16)
    preact = jnp.dot(aggregated, weight[...], preferred_element_type=F32) + bias[...]
    sig = jax.nn.sigmoid(preact)
    hidden[...] = (preact * sig).astype(BF16)
    dpreact = cotangent[...].astype(F32) * (sig * (1.0 + preact * (1.0 - sig)))
    weight_part = lax.dot_general(
        aggregated, dpreact.astype(BF16), (((0,), (0,)), ((), ())), preferred_element_type=F32
    ).astype(BF16)
    bias_part = jnp.sum(dpreact, axis=0, keepdims=True)
    rows = lax.broadcasted_iota(I32, (16, TILE), 0)
    left = jnp.broadcast_to(bias_part[:, :TILE], (16, TILE))
    right = jnp.broadcast_to(bias_part[:, TILE:], (16, TILE))
    biases = jnp.where(rows == 0, left, jnp.where(rows == 1, right, 0.0)).astype(BF16)
    for i in range(8):
        grads[i, 0:16, :] = weight_part[16 * i : 16 * i + 16, :TILE]
        grads[i, 16:32, :] = weight_part[16 * i : 16 * i + 16, TILE:]
        grads[i, 32:48, :] = biases


VMEM = pl.BlockSpec(memory_space=pltpu.VMEM)
SMEM = pl.BlockSpec(memory_space=pltpu.SMEM)
HBM = pl.BlockSpec(memory_space=pltpu.HBM)


def total(shares):
    return jnp.sum(shares.astype(F32), axis=0)


def local(features, weight, bias, cotangent, tile_values, tile_row, tile_source, tile_count, pick):
    index = lax.axis_index("wide")
    core = lax.rem(index, 2)
    both = ("wide", "narrow")
    mine = lax.dynamic_slice_in_dim(features, lax.axis_index("narrow") * (CT * TILE), CT * TILE, 0)
    own_values = tile_values[0, 0]
    other_values = lax.ppermute(own_values, "wide", OTHER_CORE)
    own = to_all(mine, "wide", FIRST).reshape(BLOCK, TILE, FIN)
    own, other_values = lax.optimization_barrier((own, other_values))
    two_a, two_b = shift(own, 2), shift(own, -2)
    one_a, one_b = shift(own, 1), shift(own, -1)
    three_a, three_b = shift(two_a, 1), shift(two_b, -1)
    four = shift(two_a, 2)

    live = jnp.arange(SLOTS, dtype=I32) < tile_count[0, 0]
    code = jnp.where(live, tile_row[0, 0] + TR * tile_source[0, 0], -1)
    first_row = jnp.arange(2, dtype=I32)[:, None] == 0
    slots = jnp.where(first_row, code[None, :], pick[0])
    other_slots = lax.ppermute(slots, "wide", OTHER_CORE)
    place = jnp.stack([core, jnp.where(core == 0, index // 16, lax.rem(index // 2, 8))])

    sums = jax.ShapeDtypeStruct((TR + 1, TILE, FIN), F32)
    here = jax.ShapeDtypeStruct(own_values.shape, BF16)
    lists = lambda n: jax.ShapeDtypeStruct((n, LIST), I32)
    starts = lambda n: jax.ShapeDtypeStruct((n, SLOTS), I32)
    own_sums, own_here, other_here, own_list, own_start = pl.pallas_call(
        own_kernel,
        out_shape=(sums, here, here, lists(1), starts(1)),
        in_specs=[SMEM, VMEM] + [HBM] * 2 + [VMEM] * 5,
        out_specs=(VMEM,) * 5,
        scratch_shapes=[
            pltpu.SMEM((1, LIST), I32),
            pltpu.SMEM((1, SLOTS), I32),
            pltpu.SemaphoreType.DMA((4,)),
        ],
        compiler_params=pltpu.CompilerParams(vmem_limit_bytes=42 << 20),
        cost_estimate=pl.CostEstimate(flops=SLOTS * TILE**3, bytes_accessed=8 << 20, transcendentals=0),
        name="own",
    )(place, slots, own_values, other_values, own, one_a, one_b, two_a, two_b)
    other_sums, all_lists, all_starts = pl.pallas_call(
        other_kernel,
        out_shape=(sums, lists(2), starts(2)),
        in_specs=[SMEM] + [VMEM] * 9,
        out_specs=(VMEM,) * 3,
        scratch_shapes=[
            pltpu.SMEM((2, LIST), I32),
            pltpu.SMEM((2, SLOTS), I32),
            pltpu.SemaphoreType.DMA((2,)),
        ],
        compiler_params=pltpu.CompilerParams(vmem_limit_bytes=16 << 20),
        cost_estimate=pl.CostEstimate(flops=SLOTS * TILE**3, bytes_accessed=8 << 20, transcendentals=0),
        name="other",
    )(place, other_slots, other_here, own_list, own_start, own, one_a, one_b, two_a, two_b)
    partial = pl.pallas_call(
        late_kernel,
        out_shape=jax.ShapeDtypeStruct((2, TR, TILE, FIN), BF16),
        in_specs=[SMEM] * 3 + [VMEM] * 7,
        out_specs=VMEM,
        scratch_shapes=[pltpu.VMEM(sums.shape, F32), pltpu.VMEM(sums.shape, F32)],
        compiler_params=pltpu.CompilerParams(vmem_limit_bytes=16 << 20),
        cost_estimate=pl.CostEstimate(flops=SLOTS * TILE**3, bytes_accessed=8 << 20, transcendentals=0),
        name="late",
    )(place, all_lists, all_starts, own_here, other_here, three_a, three_b, four, own_sums, other_sums)

    rows = TR * TILE // NARROW
    parts = lax.all_to_all(partial.reshape(8, rows, FIN), both, 0, 0, axis_index_groups=COLUMN)
    hidden, grads = pl.pallas_call(
        dense_kernel,
        out_shape=(
            jax.ShapeDtypeStruct((rows, HID), BF16),
            jax.ShapeDtypeStruct((8, 48, TILE), BF16),
        ),
        in_specs=[VMEM] * 4,
        out_specs=(VMEM, VMEM),
        compiler_params=pltpu.CompilerParams(vmem_limit_bytes=16 << 20),
        cost_estimate=pl.CostEstimate(flops=4 * rows * FIN * HID, bytes_accessed=2 << 20, transcendentals=rows * HID),
        name="dense",
    )(parts, weight, bias.reshape(1, HID), cotangent)

    share = total(lax.all_to_all(grads, both, 0, 0, axis_index_groups=COLUMN))[:40]
    share = total(to_all(share, "wide", GROUPS_Y))
    share = total(to_all(share, "wide", GROUPS_Z))
    chunk = jnp.concatenate([share[0:16], share[16:32]], axis=1)
    grad_weight = to_all(chunk, both, COLUMN).reshape(FIN, HID)
    return hidden, grad_weight, share[32:34].reshape(HID)


def solution(mesh):
    placed = (
        P("wide", None),
        P(),
        P(),
        P(("wide", "narrow"), None),
        P("wide", "narrow", None, None, None),
        P("wide", "narrow", None),
        P("wide", "narrow", None),
        P("wide", "narrow"),
        P("wide", "narrow", None),
    )
    return jax.shard_map(
        local,
        mesh=mesh,
        in_specs=placed,
        out_specs=(P(("wide", "narrow"), None), P(), P()),
        check_vma=False,
    )
```

```python
import jax
import jax.numpy as jnp
from jax import lax
from jax.experimental import pallas as pl
from jax.experimental.pallas import tpu as pltpu
from jax.sharding import PartitionSpec as P

FIN = 128
HID = 256
TILE = 128
TR = 8
CT = 2
SIDE = 8
NARROW = 4
SLOTS = 128
BLOCK = SIDE * CT
STEP = 8
SEGMENTS = 8
EARLY = 5
LIST = 256
SPARE = TR
BF16 = jnp.bfloat16
F32 = jnp.float32
I32 = jnp.int32


def wide_index(z, y, core):
    return (z * SIDE + y) * 2 + core


RANGE = range(SIDE)
ALONG_Y = [[[wide_index(z, y, c) for y in RANGE] for z in RANGE] for c in (0, 1)]
ALONG_Z = [[[wide_index(z, y, c) for z in RANGE] for y in RANGE] for c in (0, 1)]
FIRST = ALONG_Y[0] + ALONG_Z[1]
SECOND = ALONG_Z[0] + ALONG_Y[1]
COLUMN = [
    [wide_index(z, y, c) * NARROW + x for c in (0, 1) for x in range(NARROW)] for z in RANGE for y in RANGE
]
PIECES = 16
NEAR = [
    [wide_index(z, 2 * k + j, c) * NARROW + x for j in (0, 1) for c in (0, 1) for x in range(NARROW)]
    for z in RANGE
    for k in range(SIDE // 2)
]
FAR = [
    [wide_index(z, 2 * k + j, c) * NARROW + x for z in RANGE for k in range(SIDE // 2)]
    for j in (0, 1)
    for c in (0, 1)
    for x in range(NARROW)
]
OTHER_CORE = [(i, i ^ 1) for i in range(2 * SIDE * SIDE)]


def to_all(block, axes, groups):
    copies = jnp.broadcast_to(block[None], (len(groups[0]), *block.shape))
    return lax.all_to_all(copies, axes, 0, 0, axis_index_groups=groups)


def shift(block, by):
    pairs = [(line[i], line[(i + (by if i % 2 == 0 else -by)) % SIDE]) for line in SECOND for i in RANGE]
    return lax.ppermute(block, "wide", pairs)


def column(vector):
    n = vector.shape[1]
    eye = lax.broadcasted_iota(I32, (n, n), 0) == lax.broadcasted_iota(I32, (n, n), 1)
    return jnp.sum(jnp.where(eye, vector, 0), axis=1, keepdims=True)


def make_list(place, slots):
    core, at = place[0], place[1]
    code, pick = slots[0:1], slots[1:2]
    source = lax.shift_right_arithmetic(code, 3)
    valid = (code >= 0) & ((source & 1) == core)
    rows = lax.broadcasted_iota(I32, (SLOTS, SLOTS), 0)
    kinds = lax.broadcasted_iota(I32, (SLOTS, SLOTS), 1)
    lanes = lax.broadcasted_iota(I32, (1, SLOTS), 1)
    picked = jnp.sum(jnp.where(rows == source, column(pick), 0), axis=0, keepdims=True)
    z, y = lax.shift_right_arithmetic(source, 4), lax.shift_right_arithmetic(source, 1) & 7
    along, across = jnp.where(core == 0, z, y), jnp.where(core == 0, y, z)
    tile = across * 2 + picked
    ahead = jnp.where(at % 2 == 0, along - at, at - along) & 7
    segment = jnp.zeros_like(ahead)
    for kind, distance in enumerate((1, 7, 6, 2, 3, 5, 4)):
        segment = jnp.where(ahead == distance, kind + 1, segment)
    segment = jnp.where(valid, segment, SEGMENTS)
    entry = lanes + SLOTS * tile + SLOTS * BLOCK * (code & 7)
    segments = column(segment)
    sizes = jnp.sum((segments == kinds).astype(I32), axis=0, keepdims=True)
    sizes = lax.shift_right_arithmetic(sizes + STEP - 1, 3) * STEP
    size = column(jnp.where(lanes < SEGMENTS, sizes, 0))
    start = jnp.sum(jnp.where(rows < kinds, size, 0), axis=0, keepdims=True)
    earlier = (segments == segment) & (rows < kinds)
    place_of = jnp.sum(earlier.astype(I32), axis=0, keepdims=True)
    place_of += jnp.sum(jnp.where(rows == segment, column(start), 0), axis=0, keepdims=True)
    place_of = jnp.where(valid, place_of, LIST)
    spare = SLOTS * BLOCK * SPARE
    hit = column(place_of) == lax.broadcasted_iota(I32, (SLOTS, LIST), 1)
    entries = spare + jnp.sum(jnp.where(hit, column(entry) - spare, 0), axis=0, keepdims=True)
    return entries, lax.shift_right_arithmetic(start, 3)


def add_products(entries, starts, owner, values, blocks, first, acc):
    for i, block in enumerate(blocks):

        def step(k, carry, block=block):
            done = []
            for u in range(STEP):
                e = entries[owner, k * STEP + u]
                tile, row = (e >> 7) & (BLOCK - 1), e >> 11
                done.append((row, jnp.dot(values[e & (SLOTS - 1)], block[tile], preferred_element_type=F32)))
            for row, product in done:
                acc[row] += product
            return carry

        lax.fori_loop(starts[owner, first + i], starts[owner, first + i + 1], step, 0)


def own_kernel(place, slots, own, other, b0, b1, b2, b3, b4, acc, own_here, other_here, lists, starts, entries, bounds, sems):
    copies = [
        pltpu.make_async_copy(own, own_here, sems.at[0]),
        pltpu.make_async_copy(other, other_here, sems.at[1]),
    ]
    copies[0].start()
    copies[1].start()
    lists[...], starts[...] = make_list(place, slots[...])
    scalars = [
        pltpu.make_async_copy(lists, entries, sems.at[2]),
        pltpu.make_async_copy(starts, bounds, sems.at[3]),
    ]
    scalars[0].start()
    scalars[1].start()
    acc[...] = jnp.zeros_like(acc)
    scalars[0].wait()
    scalars[1].wait()
    copies[0].wait()
    add_products(entries, bounds, 0, own_here, (b0, b1, b2, b3, b4), 0, acc)
    copies[1].wait()


def other_kernel(place, slots, other, own_list, own_start, b0, b1, b2, b3, b4, acc, lists, starts, entries, bounds, sems):
    lists[0:1, :], starts[0:1, :] = own_list[...], own_start[...]
    lists[1:2, :], starts[1:2, :] = make_list(place, slots[...])
    scalars = [
        pltpu.make_async_copy(lists, entries, sems.at[0]),
        pltpu.make_async_copy(starts, bounds, sems.at[1]),
    ]
    scalars[0].start()
    scalars[1].start()
    acc[...] = jnp.zeros_like(acc)
    scalars[0].wait()
    scalars[1].wait()
    add_products(entries, bounds, 1, other, (b0, b1, b2, b3, b4), 0, acc)


def late_kernel(place, lists, starts, own, other, b5, b6, b7, own_before, other_before, out, own_acc, other_acc):
    own_acc[...] = own_before[...]
    other_acc[...] = other_before[...]
    add_products(lists, starts, 0, own, (b5, b6, b7), EARLY, own_acc)
    add_products(lists, starts, 1, other, (b5, b6, b7), EARLY, other_acc)
    core = place[0]
    out[core] = own_acc[0:TR].astype(BF16)
    out[1 - core] = other_acc[0:TR].astype(BF16)


def dense_kernel(parts, weight, bias, cotangent, hidden, grads):
    total = parts[0].astype(F32)
    for i in range(1, 8):
        total += parts[i].astype(F32)
    aggregated = total.astype(BF16)
    preact = jnp.dot(aggregated, weight[...], preferred_element_type=F32) + bias[...]
    sig = jax.nn.sigmoid(preact)
    hidden[...] = (preact * sig).astype(BF16)
    dpreact = cotangent[...].astype(F32) * (sig * (1.0 + preact * (1.0 - sig)))
    weight_part = lax.dot_general(
        aggregated, dpreact.astype(BF16), (((0,), (0,)), ((), ())), preferred_element_type=F32
    )
    bias_part = jnp.sum(dpreact, axis=0, keepdims=True)
    rows = lax.broadcasted_iota(I32, (8, TILE), 0)
    left = jnp.broadcast_to(bias_part[:, :TILE], (8, TILE))
    right = jnp.broadcast_to(bias_part[:, TILE:], (8, TILE))
    biases = jnp.where(rows == 0, left, jnp.where(rows == 1, right, 0.0))
    for i in range(PIECES):
        grads[i, 0:8, :] = weight_part[8 * i : 8 * i + 8, :TILE]
        grads[i, 8:16, :] = weight_part[8 * i : 8 * i + 8, TILE:]
        grads[i, 16:24, :] = biases


VMEM = pl.BlockSpec(memory_space=pltpu.VMEM)
SMEM = pl.BlockSpec(memory_space=pltpu.SMEM)
HBM = pl.BlockSpec(memory_space=pltpu.HBM)


def total(shares):
    return jnp.sum(shares.astype(F32), axis=0)


def local(features, weight, bias, cotangent, tile_values, tile_row, tile_source, tile_count, pick):
    index = lax.axis_index("wide")
    core = lax.rem(index, 2)
    both = ("wide", "narrow")
    mine = lax.dynamic_slice_in_dim(features, lax.axis_index("narrow") * (CT * TILE), CT * TILE, 0)
    own_values = tile_values[0, 0]
    other_values = lax.ppermute(own_values, "wide", OTHER_CORE)
    own = to_all(mine, "wide", FIRST).reshape(BLOCK, TILE, FIN)
    own, other_values = lax.optimization_barrier((own, other_values))
    two_a, two_b = shift(own, 2), shift(own, -2)
    one_a, one_b = shift(own, 1), shift(own, -1)
    three_a, three_b = shift(two_a, 1), shift(two_b, -1)
    four = shift(two_a, 2)

    live = jnp.arange(SLOTS, dtype=I32) < tile_count[0, 0]
    code = jnp.where(live, tile_row[0, 0] + TR * tile_source[0, 0], -1)
    first_row = jnp.arange(2, dtype=I32)[:, None] == 0
    slots = jnp.where(first_row, code[None, :], pick[0])
    other_slots = lax.ppermute(slots, "wide", OTHER_CORE)
    place = jnp.stack([core, jnp.where(core == 0, index // 16, lax.rem(index // 2, 8))])

    sums = jax.ShapeDtypeStruct((TR + 1, TILE, FIN), F32)
    here = jax.ShapeDtypeStruct(own_values.shape, BF16)
    lists = lambda n: jax.ShapeDtypeStruct((n, LIST), I32)
    starts = lambda n: jax.ShapeDtypeStruct((n, SLOTS), I32)
    own_sums, own_here, other_here, own_list, own_start = pl.pallas_call(
        own_kernel,
        out_shape=(sums, here, here, lists(1), starts(1)),
        in_specs=[SMEM, VMEM] + [HBM] * 2 + [VMEM] * 5,
        out_specs=(VMEM,) * 5,
        scratch_shapes=[
            pltpu.SMEM((1, LIST), I32),
            pltpu.SMEM((1, SLOTS), I32),
            pltpu.SemaphoreType.DMA((4,)),
        ],
        compiler_params=pltpu.CompilerParams(vmem_limit_bytes=42 << 20),
        cost_estimate=pl.CostEstimate(flops=SLOTS * TILE**3, bytes_accessed=8 << 20, transcendentals=0),
        name="own",
    )(place, slots, own_values, other_values, own, one_a, one_b, two_a, two_b)
    other_sums, all_lists, all_starts = pl.pallas_call(
        other_kernel,
        out_shape=(sums, lists(2), starts(2)),
        in_specs=[SMEM] + [VMEM] * 9,
        out_specs=(VMEM,) * 3,
        scratch_shapes=[
            pltpu.SMEM((2, LIST), I32),
            pltpu.SMEM((2, SLOTS), I32),
            pltpu.SemaphoreType.DMA((2,)),
        ],
        compiler_params=pltpu.CompilerParams(vmem_limit_bytes=16 << 20),
        cost_estimate=pl.CostEstimate(flops=SLOTS * TILE**3, bytes_accessed=8 << 20, transcendentals=0),
        name="other",
    )(place, other_slots, other_here, own_list, own_start, own, one_a, one_b, two_a, two_b)
    partial = pl.pallas_call(
        late_kernel,
        out_shape=jax.ShapeDtypeStruct((2, TR, TILE, FIN), BF16),
        in_specs=[SMEM] * 3 + [VMEM] * 7,
        out_specs=VMEM,
        scratch_shapes=[pltpu.VMEM(sums.shape, F32), pltpu.VMEM(sums.shape, F32)],
        compiler_params=pltpu.CompilerParams(vmem_limit_bytes=16 << 20),
        cost_estimate=pl.CostEstimate(flops=SLOTS * TILE**3, bytes_accessed=8 << 20, transcendentals=0),
        name="late",
    )(place, all_lists, all_starts, own_here, other_here, three_a, three_b, four, own_sums, other_sums)

    rows = TR * TILE // NARROW
    parts = lax.all_to_all(partial.reshape(8, rows, FIN), both, 0, 0, axis_index_groups=COLUMN)
    hidden, grads = pl.pallas_call(
        dense_kernel,
        out_shape=(
            jax.ShapeDtypeStruct((rows, HID), BF16),
            jax.ShapeDtypeStruct((PIECES, 24, TILE), F32),
        ),
        in_specs=[VMEM] * 4,
        out_specs=(VMEM, VMEM),
        compiler_params=pltpu.CompilerParams(vmem_limit_bytes=16 << 20),
        cost_estimate=pl.CostEstimate(flops=4 * rows * FIN * HID, bytes_accessed=2 << 20, transcendentals=rows * HID),
        name="dense",
    )(parts, weight, bias.reshape(1, HID), cotangent)

    share = total(lax.all_to_all(grads, both, 0, 0, axis_index_groups=NEAR)).astype(BF16)
    share = total(to_all(share, both, FAR))
    piece = jnp.concatenate([share[0:8], share[8:16]], axis=1)
    grad_weight = to_all(piece, both, NEAR).reshape(FIN, HID)
    return hidden, grad_weight, share[16:18].reshape(HID)


def solution(mesh):
    placed = (
        P("wide", None),
        P(),
        P(),
        P(("wide", "narrow"), None),
        P("wide", "narrow", None, None, None),
        P("wide", "narrow", None),
        P("wide", "narrow", None),
        P("wide", "narrow"),
        P("wide", "narrow", None),
    )
    return jax.shard_map(
        local,
        mesh=mesh,
        in_specs=placed,
        out_specs=(P(("wide", "narrow"), None), P(), P()),
        check_vma=False,
    )
```

```python
import jax
import jax.numpy as jnp
from jax import lax
from jax.experimental import pallas as pl
from jax.experimental.pallas import tpu as pltpu
from jax.sharding import PartitionSpec as P

FIN = 128
HID = 256
TILE = 128
TR = 8
CT = 2
SIDE = 8
NARROW = 4
SLOTS = 128
BLOCK = SIDE * CT
STEP = 8
SEGMENTS = 8
EARLY = 5
LAST = 7
LIST = 256
SPARE = TR
BF16 = jnp.bfloat16
F32 = jnp.float32
I32 = jnp.int32


def wide_index(z, y, core):
    return (z * SIDE + y) * 2 + core


RANGE = range(SIDE)
ALONG_Y = [[[wide_index(z, y, c) for y in RANGE] for z in RANGE] for c in (0, 1)]
ALONG_Z = [[[wide_index(z, y, c) for z in RANGE] for y in RANGE] for c in (0, 1)]
FIRST = ALONG_Z[0] + ALONG_Y[1]
SECOND = ALONG_Y[0] + ALONG_Z[1]
COLUMN = [
    [wide_index(z, y, c) * NARROW + x for c in (0, 1) for x in range(NARROW)] for z in RANGE for y in RANGE
]
PIECES = 16
NEAR = [
    [wide_index(z, 2 * k + j, c) * NARROW + x for j in (0, 1) for c in (0, 1) for x in range(NARROW)]
    for z in RANGE
    for k in range(SIDE // 2)
]
FAR = [
    [wide_index(z, 2 * k + j, c) * NARROW + x for z in RANGE for k in range(SIDE // 2)]
    for j in (0, 1)
    for c in (0, 1)
    for x in range(NARROW)
]
OTHER_CORE = [(i, i ^ 1) for i in range(2 * SIDE * SIDE)]


def to_all(block, axes, groups):
    copies = jnp.broadcast_to(block[None], (len(groups[0]), *block.shape))
    return lax.all_to_all(copies, axes, 0, 0, axis_index_groups=groups)


def shift(block, by):
    pairs = [(line[i], line[(i + (by if i % 2 == 0 else -by)) % SIDE]) for line in SECOND for i in RANGE]
    return lax.ppermute(block, "wide", pairs)


def column(vector):
    n = vector.shape[1]
    eye = lax.broadcasted_iota(I32, (n, n), 0) == lax.broadcasted_iota(I32, (n, n), 1)
    return jnp.sum(jnp.where(eye, vector, 0), axis=1, keepdims=True)


def make_list(place, slots):
    core, at = place[0], place[1]
    code, pick = slots[0:1], slots[1:2]
    source = lax.shift_right_arithmetic(code, 3)
    valid = (code >= 0) & ((source & 1) == core)
    rows = lax.broadcasted_iota(I32, (SLOTS, SLOTS), 0)
    kinds = lax.broadcasted_iota(I32, (SLOTS, SLOTS), 1)
    lanes = lax.broadcasted_iota(I32, (1, SLOTS), 1)
    picked = jnp.sum(jnp.where(rows == source, column(pick), 0), axis=0, keepdims=True)
    z, y = lax.shift_right_arithmetic(source, 4), lax.shift_right_arithmetic(source, 1) & 7
    along, across = jnp.where(core == 0, y, z), jnp.where(core == 0, z, y)
    tile = across * 2 + picked
    ahead = jnp.where(at % 2 == 0, along - at, at - along) & 7
    segment = jnp.zeros_like(ahead)
    for kind, distance in enumerate((1, 7, 6, 2, 3, 4, 5)):
        segment = jnp.where(ahead == distance, kind + 1, segment)
    segment = jnp.where(valid, segment, SEGMENTS)
    entry = lanes + SLOTS * tile + SLOTS * BLOCK * (code & 7)
    segments = column(segment)
    sizes = jnp.sum((segments == kinds).astype(I32), axis=0, keepdims=True)
    sizes = lax.shift_right_arithmetic(sizes + STEP - 1, 3) * STEP
    size = column(jnp.where(lanes < SEGMENTS, sizes, 0))
    start = jnp.sum(jnp.where(rows < kinds, size, 0), axis=0, keepdims=True)
    earlier = (segments == segment) & (rows < kinds)
    place_of = jnp.sum(earlier.astype(I32), axis=0, keepdims=True)
    place_of += jnp.sum(jnp.where(rows == segment, column(start), 0), axis=0, keepdims=True)
    place_of = jnp.where(valid, place_of, LIST)
    spare = SLOTS * BLOCK * SPARE
    hit = column(place_of) == lax.broadcasted_iota(I32, (SLOTS, LIST), 1)
    entries = spare + jnp.sum(jnp.where(hit, column(entry) - spare, 0), axis=0, keepdims=True)
    return entries, lax.shift_right_arithmetic(start, 3)


def add_products(entries, starts, owner, values, blocks, first, acc):
    for i, block in enumerate(blocks):

        def step(k, carry, block=block):
            done = []
            for u in range(STEP):
                e = entries[owner, k * STEP + u]
                tile, row = (e >> 7) & (BLOCK - 1), e >> 11
                done.append((row, jnp.dot(values[e & (SLOTS - 1)], block[tile], preferred_element_type=F32)))
            for row, product in done:
                acc[row] += product
            return carry

        lax.fori_loop(starts[owner, first + i], starts[owner, first + i + 1], step, 0)


def own_kernel(place, slots, own, b0, b1, b2, b3, b4, acc, own_here, lists, starts, entries, bounds, sems):
    copy = pltpu.make_async_copy(own, own_here, sems.at[0])
    copy.start()
    lists[...], starts[...] = make_list(place, slots[...])
    scalars = [
        pltpu.make_async_copy(lists, entries, sems.at[1]),
        pltpu.make_async_copy(starts, bounds, sems.at[2]),
    ]
    scalars[0].start()
    scalars[1].start()
    acc[...] = jnp.zeros_like(acc)
    scalars[0].wait()
    scalars[1].wait()
    copy.wait()
    add_products(entries, bounds, 0, own_here, (b0, b1, b2, b3, b4), 0, acc)


def other_kernel(
    place, slots, other, own, own_list, own_start, own_before, b0, b1, b2, b3, b4, b5, b6,
    own_acc, other_acc, other_here, lists, starts, entries, bounds, sems,
):
    copy = pltpu.make_async_copy(other, other_here, sems.at[0])
    copy.start()
    lists[0:1, :], starts[0:1, :] = own_list[...], own_start[...]
    lists[1:2, :], starts[1:2, :] = make_list(place, slots[...])
    scalars = [
        pltpu.make_async_copy(lists, entries, sems.at[1]),
        pltpu.make_async_copy(starts, bounds, sems.at[2]),
    ]
    scalars[0].start()
    scalars[1].start()
    own_acc[...] = own_before[...]
    other_acc[...] = jnp.zeros_like(other_acc)
    scalars[0].wait()
    scalars[1].wait()
    add_products(entries, bounds, 0, own, (b5, b6), EARLY, own_acc)
    copy.wait()
    add_products(entries, bounds, 1, other_here, (b0, b1, b2, b3, b4, b5, b6), 0, other_acc)


def late_kernel(place, lists, starts, own, other, b7, own_before, other_before, out, own_acc, other_acc):
    own_acc[...] = own_before[...]
    other_acc[...] = other_before[...]
    add_products(lists, starts, 0, own, (b7,), LAST, own_acc)
    add_products(lists, starts, 1, other, (b7,), LAST, other_acc)
    core = place[0]
    out[core] = own_acc[0:TR].astype(BF16)
    out[1 - core] = other_acc[0:TR].astype(BF16)


def dense_kernel(parts, weight, bias, cotangent, hidden, grads):
    total = parts[0].astype(F32)
    for i in range(1, 8):
        total += parts[i].astype(F32)
    aggregated = total.astype(BF16)
    preact = jnp.dot(aggregated, weight[...], preferred_element_type=F32) + bias[...]
    sig = jax.nn.sigmoid(preact)
    hidden[...] = (preact * sig).astype(BF16)
    dpreact = cotangent[...].astype(F32) * (sig * (1.0 + preact * (1.0 - sig)))
    weight_part = lax.dot_general(
        aggregated, dpreact.astype(BF16), (((0,), (0,)), ((), ())), preferred_element_type=F32
    )
    bias_part = jnp.sum(dpreact, axis=0, keepdims=True)
    rows = lax.broadcasted_iota(I32, (8, TILE), 0)
    left = jnp.broadcast_to(bias_part[:, :TILE], (8, TILE))
    right = jnp.broadcast_to(bias_part[:, TILE:], (8, TILE))
    biases = jnp.where(rows == 0, left, jnp.where(rows == 1, right, 0.0))
    for i in range(PIECES):
        grads[i, 0:8, :] = weight_part[8 * i : 8 * i + 8, :TILE]
        grads[i, 8:16, :] = weight_part[8 * i : 8 * i + 8, TILE:]
        grads[i, 16:24, :] = biases


VMEM = pl.BlockSpec(memory_space=pltpu.VMEM)
SMEM = pl.BlockSpec(memory_space=pltpu.SMEM)
HBM = pl.BlockSpec(memory_space=pltpu.HBM)


def total(shares):
    return jnp.sum(shares.astype(F32), axis=0)


def local(features, weight, bias, cotangent, tile_values, tile_row, tile_source, tile_count, pick):
    index = lax.axis_index("wide")
    core = lax.rem(index, 2)
    both = ("wide", "narrow")
    mine = lax.dynamic_slice_in_dim(features, lax.axis_index("narrow") * (CT * TILE), CT * TILE, 0)
    own_values = tile_values[0, 0]
    other_values = lax.ppermute(own_values, "wide", OTHER_CORE)
    own = to_all(mine, "wide", FIRST).reshape(BLOCK, TILE, FIN)
    own, other_values = lax.optimization_barrier((own, other_values))
    two_a, two_b = shift(own, 2), shift(own, -2)
    one_a, one_b = shift(own, 1), shift(own, -1)
    three_a, three_b = shift(two_a, 1), shift(two_b, -1)
    four = shift(two_a, 2)

    live = jnp.arange(SLOTS, dtype=I32) < tile_count[0, 0]
    code = jnp.where(live, tile_row[0, 0] + TR * tile_source[0, 0], -1)
    first_row = jnp.arange(2, dtype=I32)[:, None] == 0
    slots = jnp.where(first_row, code[None, :], pick[0])
    other_slots = lax.ppermute(slots, "wide", OTHER_CORE)
    place = jnp.stack([core, jnp.where(core == 0, lax.rem(index // 2, 8), index // 16)])

    sums = jax.ShapeDtypeStruct((TR + 1, TILE, FIN), F32)
    here = jax.ShapeDtypeStruct(own_values.shape, BF16)
    lists = lambda n: jax.ShapeDtypeStruct((n, LIST), I32)
    starts = lambda n: jax.ShapeDtypeStruct((n, SLOTS), I32)
    own_sums, own_here, own_list, own_start = pl.pallas_call(
        own_kernel,
        out_shape=(sums, here, lists(1), starts(1)),
        in_specs=[SMEM, VMEM, HBM] + [VMEM] * 5,
        out_specs=(VMEM,) * 4,
        scratch_shapes=[
            pltpu.SMEM((1, LIST), I32),
            pltpu.SMEM((1, SLOTS), I32),
            pltpu.SemaphoreType.DMA((3,)),
        ],
        compiler_params=pltpu.CompilerParams(vmem_limit_bytes=45 << 20),
        cost_estimate=pl.CostEstimate(flops=SLOTS * TILE**3, bytes_accessed=8 << 20, transcendentals=0),
        name="own",
    )(place, slots, own_values, own, one_a, one_b, two_a, two_b)
    own_sums, other_sums, other_here, all_lists, all_starts = pl.pallas_call(
        other_kernel,
        out_shape=(sums, sums, here, lists(2), starts(2)),
        in_specs=[SMEM, VMEM, HBM] + [VMEM] * 11,
        out_specs=(VMEM,) * 5,
        scratch_shapes=[
            pltpu.SMEM((2, LIST), I32),
            pltpu.SMEM((2, SLOTS), I32),
            pltpu.SemaphoreType.DMA((3,)),
        ],
        compiler_params=pltpu.CompilerParams(vmem_limit_bytes=24 << 20),
        cost_estimate=pl.CostEstimate(flops=SLOTS * TILE**3, bytes_accessed=8 << 20, transcendentals=0),
        name="other",
    )(
        place, other_slots, other_values, own_here, own_list, own_start, own_sums,
        own, one_a, one_b, two_a, two_b, three_a, four,
    )
    partial = pl.pallas_call(
        late_kernel,
        out_shape=jax.ShapeDtypeStruct((2, TR, TILE, FIN), BF16),
        in_specs=[SMEM] * 3 + [VMEM] * 5,
        out_specs=VMEM,
        scratch_shapes=[pltpu.VMEM(sums.shape, F32), pltpu.VMEM(sums.shape, F32)],
        compiler_params=pltpu.CompilerParams(vmem_limit_bytes=16 << 20),
        cost_estimate=pl.CostEstimate(flops=SLOTS * TILE**3, bytes_accessed=8 << 20, transcendentals=0),
        name="late",
    )(place, all_lists, all_starts, own_here, other_here, three_b, own_sums, other_sums)

    rows = TR * TILE // NARROW
    parts = lax.all_to_all(partial.reshape(8, rows, FIN), both, 0, 0, axis_index_groups=COLUMN)
    hidden, grads = pl.pallas_call(
        dense_kernel,
        out_shape=(
            jax.ShapeDtypeStruct((rows, HID), BF16),
            jax.ShapeDtypeStruct((PIECES, 24, TILE), F32),
        ),
        in_specs=[VMEM] * 4,
        out_specs=(VMEM, VMEM),
        compiler_params=pltpu.CompilerParams(vmem_limit_bytes=16 << 20),
        cost_estimate=pl.CostEstimate(flops=4 * rows * FIN * HID, bytes_accessed=2 << 20, transcendentals=rows * HID),
        name="dense",
    )(parts, weight, bias.reshape(1, HID), cotangent)

    share = total(lax.all_to_all(grads, both, 0, 0, axis_index_groups=NEAR)).astype(BF16)
    share = total(to_all(share, both, FAR))
    piece = jnp.concatenate([share[0:8], share[8:16]], axis=1)
    piece, grad_bias = lax.optimization_barrier((piece, share[16:18].reshape(HID)))
    grad_weight = to_all(piece, both, NEAR).reshape(FIN, HID)
    return hidden, grad_weight, grad_bias


def solution(mesh):
    placed = (
        P("wide", None),
        P(),
        P(),
        P(("wide", "narrow"), None),
        P("wide", "narrow", None, None, None),
        P("wide", "narrow", None),
        P("wide", "narrow", None),
        P("wide", "narrow"),
        P("wide", "narrow", None),
    )
    return jax.shard_map(
        local,
        mesh=mesh,
        in_specs=placed,
        out_specs=(P(("wide", "narrow"), None), P(), P()),
        check_vma=False,
    )
```

```python
import jax
import jax.numpy as jnp
from jax import lax
from jax.experimental import pallas as pl
from jax.experimental.pallas import tpu as pltpu
from jax.sharding import PartitionSpec as P

FIN = 128
HID = 256
TILE = 128
TR = 8
CT = 2
SIDE = 8
NARROW = 4
SLOTS = 128
BLOCK = SIDE * CT
STEP = 4
SEGMENTS = 8
EARLY = 5
LAST = 7
LIST = 256
SPARE = TR
BF16 = jnp.bfloat16
F32 = jnp.float32
I32 = jnp.int32


def wide_index(z, y, core):
    return (z * SIDE + y) * 2 + core


RANGE = range(SIDE)
ALONG_Y = [[[wide_index(z, y, c) for y in RANGE] for z in RANGE] for c in (0, 1)]
ALONG_Z = [[[wide_index(z, y, c) for z in RANGE] for y in RANGE] for c in (0, 1)]
FIRST = ALONG_Z[0] + ALONG_Y[1]
SECOND = ALONG_Y[0] + ALONG_Z[1]
COLUMN = [
    [wide_index(z, y, c) * NARROW + x for c in (0, 1) for x in range(NARROW)] for z in RANGE for y in RANGE
]
PIECES = 16
NEAR = [
    [wide_index(z, 2 * k + j, c) * NARROW + x for j in (0, 1) for c in (0, 1) for x in range(NARROW)]
    for z in RANGE
    for k in range(SIDE // 2)
]
FAR = [
    [wide_index(z, 2 * k + j, c) * NARROW + x for z in RANGE for k in range(SIDE // 2)]
    for j in (0, 1)
    for c in (0, 1)
    for x in range(NARROW)
]
OTHER_CORE = [(i, i ^ 1) for i in range(2 * SIDE * SIDE)]


def to_all(block, axes, groups):
    copies = jnp.broadcast_to(block[None], (len(groups[0]), *block.shape))
    return lax.all_to_all(copies, axes, 0, 0, axis_index_groups=groups)


def shift(block, by):
    pairs = [(line[i], line[(i + (by if i % 2 == 0 else -by)) % SIDE]) for line in SECOND for i in RANGE]
    return lax.ppermute(block, "wide", pairs)


def column(vector):
    n = vector.shape[1]
    eye = lax.broadcasted_iota(I32, (n, n), 0) == lax.broadcasted_iota(I32, (n, n), 1)
    return jnp.sum(jnp.where(eye, vector, 0), axis=1, keepdims=True)


def make_list(place, slots):
    core, at = place[0], place[1]
    code, pick = slots[0:1], slots[1:2]
    source = lax.shift_right_arithmetic(code, 3)
    valid = (code >= 0) & ((source & 1) == core)
    rows = lax.broadcasted_iota(I32, (SLOTS, SLOTS), 0)
    kinds = lax.broadcasted_iota(I32, (SLOTS, SLOTS), 1)
    lanes = lax.broadcasted_iota(I32, (1, SLOTS), 1)
    picked = jnp.sum(jnp.where(rows == source, column(pick), 0), axis=0, keepdims=True)
    z, y = lax.shift_right_arithmetic(source, 4), lax.shift_right_arithmetic(source, 1) & 7
    along, across = jnp.where(core == 0, y, z), jnp.where(core == 0, z, y)
    tile = across * 2 + picked
    ahead = jnp.where(at % 2 == 0, along - at, at - along) & 7
    segment = jnp.zeros_like(ahead)
    for kind, distance in enumerate((1, 7, 6, 2, 3, 4, 5)):
        segment = jnp.where(ahead == distance, kind + 1, segment)
    segment = jnp.where(valid, segment, SEGMENTS)
    entry = lanes + SLOTS * tile + SLOTS * BLOCK * (code & 7)
    segments = column(segment)
    sizes = jnp.sum((segments == kinds).astype(I32), axis=0, keepdims=True)
    sizes = lax.shift_right_arithmetic(sizes + STEP - 1, 2) * STEP
    size = column(jnp.where(lanes < SEGMENTS, sizes, 0))
    start = jnp.sum(jnp.where(rows < kinds, size, 0), axis=0, keepdims=True)
    earlier = (segments == segment) & (rows < kinds)
    place_of = jnp.sum(earlier.astype(I32), axis=0, keepdims=True)
    place_of += jnp.sum(jnp.where(rows == segment, column(start), 0), axis=0, keepdims=True)
    place_of = jnp.where(valid, place_of, LIST)
    spare = SLOTS * BLOCK * SPARE
    hit = column(place_of) == lax.broadcasted_iota(I32, (SLOTS, LIST), 1)
    entries = spare + jnp.sum(jnp.where(hit, column(entry) - spare, 0), axis=0, keepdims=True)
    return entries, lax.shift_right_arithmetic(start, 2)


def add_products(entries, starts, owner, values, blocks, first, acc):
    for i, block in enumerate(blocks):
        begin, end = starts[owner, first + i], starts[owner, first + i + 1]

        def add(at, n, block=block):
            done = []
            for u in range(n):
                e = entries[owner, at + u]
                tile, row = (e >> 7) & (BLOCK - 1), e >> 11
                done.append((row, jnp.dot(values[e & (SLOTS - 1)], block[tile], preferred_element_type=F32)))
            for row, product in done:
                acc[row] += product

        def two(k, carry, begin=begin, add=add):
            add((begin + 2 * k) * STEP, 2 * STEP)
            return carry

        def one(k, carry, end=end, add=add):
            add((end - 1) * STEP, STEP)
            return carry

        lax.fori_loop(0, (end - begin) >> 1, two, 0)
        lax.fori_loop(0, (end - begin) & 1, one, 0)


def own_kernel(
    place, slots, own, other, b0, b1, b2, b3, b4,
    acc, own_here, other_here, lists, starts, entries, bounds, sems,
):
    copy = pltpu.make_async_copy(own, own_here, sems.at[0])
    other_copy = pltpu.make_async_copy(other, other_here, sems.at[3])
    copy.start()
    other_copy.start()
    lists[...], starts[...] = make_list(place, slots[...])
    scalars = [
        pltpu.make_async_copy(lists, entries, sems.at[1]),
        pltpu.make_async_copy(starts, bounds, sems.at[2]),
    ]
    scalars[0].start()
    scalars[1].start()
    acc[...] = jnp.zeros_like(acc)
    scalars[0].wait()
    scalars[1].wait()
    copy.wait()
    add_products(entries, bounds, 0, own_here, (b0, b1, b2, b3, b4), 0, acc)
    other_copy.wait()


def other_kernel(
    place, slots, other, own, own_list, own_start, own_before, b0, b1, b2, b3, b4, b5, b6,
    own_acc, other_acc, lists, starts, entries, bounds, sems,
):
    lists[0:1, :], starts[0:1, :] = own_list[...], own_start[...]
    lists[1:2, :], starts[1:2, :] = make_list(place, slots[...])
    scalars = [
        pltpu.make_async_copy(lists, entries, sems.at[0]),
        pltpu.make_async_copy(starts, bounds, sems.at[1]),
    ]
    scalars[0].start()
    scalars[1].start()
    own_acc[...] = own_before[...]
    other_acc[...] = jnp.zeros_like(other_acc)
    scalars[0].wait()
    scalars[1].wait()
    add_products(entries, bounds, 0, own, (b5, b6), EARLY, own_acc)
    add_products(entries, bounds, 1, other, (b0, b1, b2, b3, b4, b5, b6), 0, other_acc)


def late_kernel(place, lists, starts, own, other, b7, own_before, other_before, out, own_acc, other_acc):
    own_acc[...] = own_before[...]
    other_acc[...] = other_before[...]
    add_products(lists, starts, 0, own, (b7,), LAST, own_acc)
    add_products(lists, starts, 1, other, (b7,), LAST, other_acc)
    core = place[0]
    out[core] = own_acc[0:TR].astype(BF16)
    out[1 - core] = other_acc[0:TR].astype(BF16)


def dense_kernel(parts, weight, bias, cotangent, hidden, grads):
    total = parts[0].astype(F32)
    for i in range(1, 8):
        total += parts[i].astype(F32)
    aggregated = total.astype(BF16)
    preact = jnp.dot(aggregated, weight[...], preferred_element_type=F32) + bias[...]
    sig = jax.nn.sigmoid(preact)
    hidden[...] = (preact * sig).astype(BF16)
    dpreact = cotangent[...].astype(F32) * (sig * (1.0 + preact * (1.0 - sig)))
    weight_part = lax.dot_general(
        aggregated, dpreact.astype(BF16), (((0,), (0,)), ((), ())), preferred_element_type=F32
    )
    bias_part = jnp.sum(dpreact, axis=0, keepdims=True)
    rows = lax.broadcasted_iota(I32, (8, TILE), 0)
    left = jnp.broadcast_to(bias_part[:, :TILE], (8, TILE))
    right = jnp.broadcast_to(bias_part[:, TILE:], (8, TILE))
    biases = jnp.where(rows == 0, left, jnp.where(rows == 1, right, 0.0))
    for i in range(PIECES):
        grads[i, 0:8, :] = weight_part[8 * i : 8 * i + 8, :TILE]
        grads[i, 8:16, :] = weight_part[8 * i : 8 * i + 8, TILE:]
        grads[i, 16:24, :] = biases


VMEM = pl.BlockSpec(memory_space=pltpu.VMEM)
SMEM = pl.BlockSpec(memory_space=pltpu.SMEM)
HBM = pl.BlockSpec(memory_space=pltpu.HBM)


def total(shares):
    return jnp.sum(shares.astype(F32), axis=0)


def local(features, weight, bias, cotangent, tile_values, tile_row, tile_source, tile_count, pick):
    index = lax.axis_index("wide")
    core = lax.rem(index, 2)
    both = ("wide", "narrow")
    mine = lax.dynamic_slice_in_dim(features, lax.axis_index("narrow") * (CT * TILE), CT * TILE, 0)
    own_values = tile_values[0, 0]
    other_values = lax.ppermute(own_values, "wide", OTHER_CORE)
    own = to_all(mine, "wide", FIRST).reshape(BLOCK, TILE, FIN)
    own, other_values = lax.optimization_barrier((own, other_values))
    two_a, two_b = shift(own, 2), shift(own, -2)
    one_a, one_b = shift(own, 1), shift(own, -1)
    three_a, three_b = shift(two_a, 1), shift(two_b, -1)
    four = shift(two_a, 2)

    live = jnp.arange(SLOTS, dtype=I32) < tile_count[0, 0]
    code = jnp.where(live, tile_row[0, 0] + TR * tile_source[0, 0], -1)
    first_row = jnp.arange(2, dtype=I32)[:, None] == 0
    slots = jnp.where(first_row, code[None, :], pick[0])
    other_slots = lax.ppermute(slots, "wide", OTHER_CORE)
    place = jnp.stack([core, jnp.where(core == 0, lax.rem(index // 2, 8), index // 16)])

    sums = jax.ShapeDtypeStruct((TR + 1, TILE, FIN), F32)
    here = jax.ShapeDtypeStruct(own_values.shape, BF16)
    lists = lambda n: jax.ShapeDtypeStruct((n, LIST), I32)
    starts = lambda n: jax.ShapeDtypeStruct((n, SLOTS), I32)
    own_sums, own_here, other_here, own_list, own_start = pl.pallas_call(
        own_kernel,
        out_shape=(sums, here, here, lists(1), starts(1)),
        in_specs=[SMEM, VMEM] + [HBM] * 2 + [VMEM] * 5,
        out_specs=(VMEM,) * 5,
        scratch_shapes=[
            pltpu.SMEM((1, LIST), I32),
            pltpu.SMEM((1, SLOTS), I32),
            pltpu.SemaphoreType.DMA((4,)),
        ],
        compiler_params=pltpu.CompilerParams(vmem_limit_bytes=41 << 20),
        cost_estimate=pl.CostEstimate(flops=SLOTS * TILE**3, bytes_accessed=8 << 20, transcendentals=0),
        name="own",
    )(place, slots, own_values, other_values, own, one_a, one_b, two_a, two_b)
    own_sums, other_sums, all_lists, all_starts = pl.pallas_call(
        other_kernel,
        out_shape=(sums, sums, lists(2), starts(2)),
        in_specs=[SMEM] + [VMEM] * 13,
        out_specs=(VMEM,) * 4,
        scratch_shapes=[
            pltpu.SMEM((2, LIST), I32),
            pltpu.SMEM((2, SLOTS), I32),
            pltpu.SemaphoreType.DMA((2,)),
        ],
        compiler_params=pltpu.CompilerParams(vmem_limit_bytes=24 << 20),
        cost_estimate=pl.CostEstimate(flops=SLOTS * TILE**3, bytes_accessed=8 << 20, transcendentals=0),
        name="other",
    )(
        place, other_slots, other_here, own_here, own_list, own_start, own_sums,
        own, one_a, one_b, two_a, two_b, three_a, four,
    )
    partial = pl.pallas_call(
        late_kernel,
        out_shape=jax.ShapeDtypeStruct((2, TR, TILE, FIN), BF16),
        in_specs=[SMEM] * 3 + [VMEM] * 5,
        out_specs=VMEM,
        scratch_shapes=[pltpu.VMEM(sums.shape, F32), pltpu.VMEM(sums.shape, F32)],
        compiler_params=pltpu.CompilerParams(vmem_limit_bytes=16 << 20),
        cost_estimate=pl.CostEstimate(flops=SLOTS * TILE**3, bytes_accessed=8 << 20, transcendentals=0),
        name="late",
    )(place, all_lists, all_starts, own_here, other_here, three_b, own_sums, other_sums)

    rows = TR * TILE // NARROW
    parts = lax.all_to_all(partial.reshape(8, rows, FIN), both, 0, 0, axis_index_groups=COLUMN)
    hidden, grads = pl.pallas_call(
        dense_kernel,
        out_shape=(
            jax.ShapeDtypeStruct((rows, HID), BF16),
            jax.ShapeDtypeStruct((PIECES, 24, TILE), F32),
        ),
        in_specs=[VMEM] * 4,
        out_specs=(VMEM, VMEM),
        compiler_params=pltpu.CompilerParams(vmem_limit_bytes=16 << 20),
        cost_estimate=pl.CostEstimate(flops=4 * rows * FIN * HID, bytes_accessed=2 << 20, transcendentals=rows * HID),
        name="dense",
    )(parts, weight, bias.reshape(1, HID), cotangent)

    share = total(lax.all_to_all(grads.astype(BF16), both, 0, 0, axis_index_groups=NEAR)).astype(BF16)
    share = total(to_all(share, both, FAR))
    piece = jnp.concatenate([share[0:8], share[8:16]], axis=1)
    piece, grad_bias = lax.optimization_barrier((piece, share[16:18].reshape(HID)))
    grad_weight = to_all(piece, both, NEAR).reshape(FIN, HID)
    return hidden, grad_weight, grad_bias


def solution(mesh):
    placed = (
        P("wide", None),
        P(),
        P(),
        P(("wide", "narrow"), None),
        P("wide", "narrow", None, None, None),
        P("wide", "narrow", None),
        P("wide", "narrow", None),
        P("wide", "narrow"),
        P("wide", "narrow", None),
    )
    return jax.shard_map(
        local,
        mesh=mesh,
        in_specs=placed,
        out_specs=(P(("wide", "narrow"), None), P(), P()),
        check_vma=False,
    )
```

```python
import jax
import jax.numpy as jnp
from jax import lax
from jax.experimental import pallas as pl
from jax.experimental.pallas import tpu as pltpu
from jax.sharding import PartitionSpec as P

FIN = 128
HID = 256
TILE = 128
TR = 8
CT = 2
SIDE = 8
NARROW = 4
SLOTS = 128
BLOCK = SIDE * CT
STEP = 4
SEGMENTS = 8
EARLY = 5
LAST = 7
LIST = 256
SPARE = TR
BF16 = jnp.bfloat16
F32 = jnp.float32
I32 = jnp.int32


def wide_index(z, y, core):
    return (z * SIDE + y) * 2 + core


RANGE = range(SIDE)
ALONG_Y = [[[wide_index(z, y, c) for y in RANGE] for z in RANGE] for c in (0, 1)]
ALONG_Z = [[[wide_index(z, y, c) for z in RANGE] for y in RANGE] for c in (0, 1)]
FIRST = ALONG_Z[0] + ALONG_Y[1]
SECOND = ALONG_Y[0] + ALONG_Z[1]
COLUMN = [
    [wide_index(z, y, c) * NARROW + x for c in (0, 1) for x in range(NARROW)] for z in RANGE for y in RANGE
]
PIECES = 16
NEAR = [
    [wide_index(z, 2 * k + j, c) * NARROW + x for j in (0, 1) for c in (0, 1) for x in range(NARROW)]
    for z in RANGE
    for k in range(SIDE // 2)
]
FAR = [
    [wide_index(z, 2 * k + j, c) * NARROW + x for z in RANGE for k in range(SIDE // 2)]
    for j in (0, 1)
    for c in (0, 1)
    for x in range(NARROW)
]
OTHER_CORE = [(i, i ^ 1) for i in range(2 * SIDE * SIDE)]


def to_all(block, axes, groups):
    copies = jnp.broadcast_to(block[None], (len(groups[0]), *block.shape))
    return lax.all_to_all(copies, axes, 0, 0, axis_index_groups=groups)


def shift(block, by):
    pairs = [(line[i], line[(i + (by if i % 2 == 0 else -by)) % SIDE]) for line in SECOND for i in RANGE]
    return lax.ppermute(block, "wide", pairs)


def column(vector):
    n = vector.shape[1]
    eye = lax.broadcasted_iota(I32, (n, n), 0) == lax.broadcasted_iota(I32, (n, n), 1)
    return jnp.sum(jnp.where(eye, vector, 0), axis=1, keepdims=True)


def make_list(place, slots):
    core, at = place[0], place[1]
    code = slots
    source = lax.shift_right_arithmetic(code, 3) & (SLOTS - 1)
    pick = lax.shift_right_arithmetic(code, 10) & 1
    valid = (code < 2048) & ((source & 1) == core)
    rows = lax.broadcasted_iota(I32, (SLOTS, SLOTS), 0)
    kinds = lax.broadcasted_iota(I32, (SLOTS, SLOTS), 1)
    lanes = lax.broadcasted_iota(I32, (1, SLOTS), 1)
    picked = jnp.sum(jnp.where(rows == source, column(pick), 0), axis=0, keepdims=True)
    z, y = lax.shift_right_arithmetic(source, 4), lax.shift_right_arithmetic(source, 1) & 7
    along, across = jnp.where(core == 0, y, z), jnp.where(core == 0, z, y)
    tile = across * 2 + picked
    ahead = jnp.where(at % 2 == 0, along - at, at - along) & 7
    segment = jnp.zeros_like(ahead)
    for kind, distance in enumerate((1, 7, 6, 2, 3, 4, 5)):
        segment = jnp.where(ahead == distance, kind + 1, segment)
    segment = jnp.where(valid, segment, SEGMENTS)
    entry = lanes + SLOTS * tile + SLOTS * BLOCK * (code & 7)
    segments = column(segment)
    sizes = jnp.sum((segments == kinds).astype(I32), axis=0, keepdims=True)
    sizes = lax.shift_right_arithmetic(sizes + STEP - 1, 2) * STEP
    size = column(jnp.where(lanes < SEGMENTS, sizes, 0))
    start = jnp.sum(jnp.where(rows < kinds, size, 0), axis=0, keepdims=True)
    earlier = (segments == segment) & (rows < kinds)
    place_of = jnp.sum(earlier.astype(I32), axis=0, keepdims=True)
    place_of += jnp.sum(jnp.where(rows == segment, column(start), 0), axis=0, keepdims=True)
    place_of = jnp.where(valid, place_of, LIST)
    spare = SLOTS * BLOCK * SPARE
    hit = column(place_of) == lax.broadcasted_iota(I32, (SLOTS, LIST), 1)
    entries = spare + jnp.sum(jnp.where(hit, column(entry) - spare, 0), axis=0, keepdims=True)
    return entries, lax.shift_right_arithmetic(start, 2)


def add_products(entries, starts, owner, values, blocks, first, acc):
    for i, block in enumerate(blocks):
        begin, end = starts[owner, first + i], starts[owner, first + i + 1]

        def add(at, n, block=block):
            done = []
            for u in range(n):
                e = entries[owner, at + u]
                tile, row = (e >> 7) & (BLOCK - 1), e >> 11
                done.append((row, jnp.dot(values[e & (SLOTS - 1)], block[tile], preferred_element_type=F32)))
            for row, product in done:
                acc[row] += product

        def two(k, carry, begin=begin, add=add):
            add((begin + 2 * k) * STEP, 2 * STEP)
            return carry

        def one(k, carry, end=end, add=add):
            add((end - 1) * STEP, STEP)
            return carry

        lax.fori_loop(0, (end - begin) >> 1, two, 0)
        lax.fori_loop(0, (end - begin) & 1, one, 0)


def own_kernel(
    place, slots, own, other, b0, b1, b2, b3, b4,
    acc, own_here, other_here, lists, starts, entries, bounds, sems,
):
    copy = pltpu.make_async_copy(own, own_here, sems.at[0])
    other_copy = pltpu.make_async_copy(other, other_here, sems.at[3])
    copy.start()
    other_copy.start()
    lists[...], starts[...] = make_list(place, slots[...])
    scalars = [
        pltpu.make_async_copy(lists, entries, sems.at[1]),
        pltpu.make_async_copy(starts, bounds, sems.at[2]),
    ]
    scalars[0].start()
    scalars[1].start()
    acc[...] = jnp.zeros_like(acc)
    scalars[0].wait()
    scalars[1].wait()
    copy.wait()
    add_products(entries, bounds, 0, own_here, (b0, b1, b2, b3, b4), 0, acc)
    other_copy.wait()


def other_kernel(
    place, slots, other, own, own_list, own_start, own_before, b0, b1, b2, b3, b4, b5, b6,
    own_acc, other_acc, lists, starts, entries, bounds, sems,
):
    lists[0:1, :], starts[0:1, :] = own_list[...], own_start[...]
    lists[1:2, :], starts[1:2, :] = make_list(place, slots[...])
    scalars = [
        pltpu.make_async_copy(lists, entries, sems.at[0]),
        pltpu.make_async_copy(starts, bounds, sems.at[1]),
    ]
    scalars[0].start()
    scalars[1].start()
    own_acc[...] = own_before[...]
    other_acc[...] = jnp.zeros_like(other_acc)
    scalars[0].wait()
    scalars[1].wait()
    add_products(entries, bounds, 0, own, (b5, b6), EARLY, own_acc)
    add_products(entries, bounds, 1, other, (b0, b1, b2, b3, b4, b5, b6), 0, other_acc)


def late_kernel(place, lists, starts, own, other, b7, own_before, other_before, out, own_acc, other_acc):
    own_acc[...] = own_before[...]
    other_acc[...] = other_before[...]
    add_products(lists, starts, 0, own, (b7,), LAST, own_acc)
    add_products(lists, starts, 1, other, (b7,), LAST, other_acc)
    core = place[0]
    out[core] = own_acc[0:TR].astype(BF16)
    out[1 - core] = other_acc[0:TR].astype(BF16)


def dense_kernel(parts, weight, bias, cotangent, hidden, grads):
    total = parts[0].astype(F32)
    for i in range(1, 8):
        total += parts[i].astype(F32)
    aggregated = total.astype(BF16)
    preact = jnp.dot(aggregated, weight[...], preferred_element_type=F32) + bias[...]
    sig = jax.nn.sigmoid(preact)
    hidden[...] = (preact * sig).astype(BF16)
    dpreact = cotangent[...].astype(F32) * (sig * (1.0 + preact * (1.0 - sig)))
    weight_part = lax.dot_general(
        aggregated, dpreact.astype(BF16), (((0,), (0,)), ((), ())), preferred_element_type=F32
    )
    bias_part = jnp.sum(dpreact, axis=0, keepdims=True)
    rows = lax.broadcasted_iota(I32, (8, TILE), 0)
    left = jnp.broadcast_to(bias_part[:, :TILE], (8, TILE))
    right = jnp.broadcast_to(bias_part[:, TILE:], (8, TILE))
    biases = jnp.where(rows == 0, left, jnp.where(rows == 1, right, 0.0))
    for i in range(PIECES):
        grads[i, 0:8, :] = weight_part[8 * i : 8 * i + 8, :TILE]
        grads[i, 8:16, :] = weight_part[8 * i : 8 * i + 8, TILE:]
        grads[i, 16:24, :] = biases


VMEM = pl.BlockSpec(memory_space=pltpu.VMEM)
SMEM = pl.BlockSpec(memory_space=pltpu.SMEM)
HBM = pl.BlockSpec(memory_space=pltpu.HBM)


def total(shares):
    return jnp.sum(shares.astype(F32), axis=0)


def local(features, weight, bias, cotangent, tile_values, tile_row, tile_source, tile_count, pick):
    index = lax.axis_index("wide")
    core = lax.rem(index, 2)
    both = ("wide", "narrow")
    mine = lax.dynamic_slice_in_dim(features, lax.axis_index("narrow") * (CT * TILE), CT * TILE, 0)
    own_values = tile_values[0, 0]
    other_values = lax.ppermute(own_values, "wide", OTHER_CORE)
    own = to_all(mine, "wide", FIRST).reshape(BLOCK, TILE, FIN)
    own, other_values = lax.optimization_barrier((own, other_values))
    two_a, two_b = shift(own, 2), shift(own, -2)
    one_a, one_b = shift(own, 1), shift(own, -1)
    three_a, three_b = shift(two_a, 1), shift(two_b, -1)
    four = shift(two_a, 2)

    live = jnp.arange(SLOTS, dtype=I32) < tile_count[0, 0]
    slots = (tile_row[0] + TR * tile_source[0]) + (1024 * pick[0] + jnp.where(live, 0, 2048)[None])
    other_slots = lax.ppermute(slots, "wide", OTHER_CORE)
    place = jnp.stack([core, jnp.where(core == 0, lax.rem(index // 2, 8), index // 16)])

    sums = jax.ShapeDtypeStruct((TR + 1, TILE, FIN), F32)
    here = jax.ShapeDtypeStruct(own_values.shape, BF16)
    lists = lambda n: jax.ShapeDtypeStruct((n, LIST), I32)
    starts = lambda n: jax.ShapeDtypeStruct((n, SLOTS), I32)
    own_sums, own_here, other_here, own_list, own_start = pl.pallas_call(
        own_kernel,
        out_shape=(sums, here, here, lists(1), starts(1)),
        in_specs=[SMEM, VMEM] + [HBM] * 2 + [VMEM] * 5,
        out_specs=(VMEM,) * 5,
        scratch_shapes=[
            pltpu.SMEM((1, LIST), I32),
            pltpu.SMEM((1, SLOTS), I32),
            pltpu.SemaphoreType.DMA((4,)),
        ],
        compiler_params=pltpu.CompilerParams(vmem_limit_bytes=41 << 20),
        cost_estimate=pl.CostEstimate(flops=SLOTS * TILE**3, bytes_accessed=8 << 20, transcendentals=0),
        name="own",
    )(place, slots, own_values, other_values, own, one_a, one_b, two_a, two_b)
    own_sums, other_sums, all_lists, all_starts = pl.pallas_call(
        other_kernel,
        out_shape=(sums, sums, lists(2), starts(2)),
        in_specs=[SMEM] + [VMEM] * 13,
        out_specs=(VMEM,) * 4,
        scratch_shapes=[
            pltpu.SMEM((2, LIST), I32),
            pltpu.SMEM((2, SLOTS), I32),
            pltpu.SemaphoreType.DMA((2,)),
        ],
        compiler_params=pltpu.CompilerParams(vmem_limit_bytes=24 << 20),
        cost_estimate=pl.CostEstimate(flops=SLOTS * TILE**3, bytes_accessed=8 << 20, transcendentals=0),
        name="other",
    )(
        place, other_slots, other_here, own_here, own_list, own_start, own_sums,
        own, one_a, one_b, two_a, two_b, three_a, four,
    )
    partial = pl.pallas_call(
        late_kernel,
        out_shape=jax.ShapeDtypeStruct((2, TR, TILE, FIN), BF16),
        in_specs=[SMEM] * 3 + [VMEM] * 5,
        out_specs=VMEM,
        scratch_shapes=[pltpu.VMEM(sums.shape, F32), pltpu.VMEM(sums.shape, F32)],
        compiler_params=pltpu.CompilerParams(vmem_limit_bytes=16 << 20),
        cost_estimate=pl.CostEstimate(flops=SLOTS * TILE**3, bytes_accessed=8 << 20, transcendentals=0),
        name="late",
    )(place, all_lists, all_starts, own_here, other_here, three_b, own_sums, other_sums)

    rows = TR * TILE // NARROW
    parts = lax.all_to_all(partial.reshape(8, rows, FIN), both, 0, 0, axis_index_groups=COLUMN)
    hidden, grads = pl.pallas_call(
        dense_kernel,
        out_shape=(
            jax.ShapeDtypeStruct((rows, HID), BF16),
            jax.ShapeDtypeStruct((PIECES, 24, TILE), F32),
        ),
        in_specs=[VMEM] * 4,
        out_specs=(VMEM, VMEM),
        compiler_params=pltpu.CompilerParams(vmem_limit_bytes=16 << 20),
        cost_estimate=pl.CostEstimate(flops=4 * rows * FIN * HID, bytes_accessed=2 << 20, transcendentals=rows * HID),
        name="dense",
    )(parts, weight, bias.reshape(1, HID), cotangent)

    share = total(lax.all_to_all(grads.astype(BF16), both, 0, 0, axis_index_groups=NEAR)).astype(BF16)
    share = total(to_all(share, both, FAR))
    piece = jnp.concatenate([share[0:8], share[8:16]], axis=1)
    piece, grad_bias = lax.optimization_barrier((piece, share[16:18].reshape(HID)))
    grad_weight = to_all(piece, both, NEAR).reshape(FIN, HID)
    return hidden, grad_weight, grad_bias


def solution(mesh):
    placed = (
        P("wide", None),
        P(),
        P(),
        P(("wide", "narrow"), None),
        P("wide", "narrow", None, None, None),
        P("wide", "narrow", None),
        P("wide", "narrow", None),
        P("wide", "narrow"),
        P("wide", "narrow", None),
    )
    return jax.shard_map(
        local,
        mesh=mesh,
        in_specs=placed,
        out_specs=(P(("wide", "narrow"), None), P(), P()),
        check_vma=False,
    )
```
